32 devices in a mesh: seq: 8 (over z, y), head: 4 (over x, core).
Axes of the slice: x: 2, y: 2, z: 4, core: 2. Of those that a mesh axis runs over, the one named last changes fastest.
Arguments:
- inputs: bfloat16 [8192, 5120], P('seq', 'head'), may hold values from -0.59765625 to 0.59765625
- gates: bfloat16 [8192, 5120], P('seq', 'head'), may hold values from -6 to 6
- write_keys: bfloat16 [8192, 128], P('seq'), may hold values from -6 to 6
- read_keys: bfloat16 [8192, 128], P('seq'), may hold values from -0.125 to 0.125
- log_decay: float32 [80, 8192], P('head', 'seq'), may hold values from -3 to 0
- skip_gain: float32 [80], P('head'), may hold values from 0.5 to 4
- doc_ids: int32 [8192], P('seq'), may hold values from 0 to 3, never falling along the last dimension, each value on 1 to 4096 neighbouring positions
- out_weight: bfloat16 [5120, 2560], P('head'), may hold values from -0.078125 to 0.078125
- grad_out: bfloat16 [8192, 2560], P(('seq', 'head')), may hold values from -6 to 6
Outputs:
- mixed_out: bfloat16 [8192, 2560], P(('seq', 'head'))
- grad_inputs: bfloat16 [8192, 5120], P('seq', 'head')
The draws below stay inside these ranges and needn't reach their ends.
Inputs may be any that keep to these rules, and one draw needn't show every extreme that they name: `doc_ids`: document ids never fall along the sequence; every document has 1 to 4096 tokens and one has exactly 4096.
All inputs are finite; a program needn't handle non-finite values.
Results may differ from the reference program's by a relative error of at most 0.02.
Values may be sent and summed in bfloat16 or wider, within the bound.
No kernel may reach another device: no remote copies, remote signals or barrier semaphores. Data moves between devices by JAX's collectives and lax.ppermute only.
A program may use at most 128 MiB of HBM per device.

```python
import math
import jax
import jax.numpy as jnp
import numpy as np
from jax import lax

D = 2560
H = 80
P_SIZE = 64
N = 128
GROUP = 256
TOK_DEV = 1024
DOCS = 4
PACKED_TOKENS = 8192


def draw_log_decay(key, part):
    key_rows = jax.random.split(key, 7)
    slow_share = 0.5
    slow_heads = jax.random.uniform(key_rows[0], (H,)) < slow_share
    fast_rate = jnp.exp(jax.random.uniform(key_rows[1], (H,), minval=math.log(1.0 / 50.0), maxval=math.log(1.0 / 30.0)))
    slow_rate = jnp.exp(jax.random.uniform(key_rows[2], (H,), minval=math.log(0.2), maxval=math.log(0.8))) / PACKED_TOKENS
    head_decay_rate = jnp.where(slow_heads, slow_rate, fast_rate)
    shard_factor = jax.random.uniform(key_rows[3], (H, PACKED_TOKENS // TOK_DEV), minval=0.6, maxval=1.4)
    shard_complete = jnp.repeat(shard_factor, TOK_DEV, axis=1)
    token_multiplier = jax.random.uniform(key_rows[4], (H, PACKED_TOKENS), minval=0.5, maxval=1.5)
    segment_location = jax.random.randint(key_rows[5], (4,), 0, PACKED_TOKENS)
    segment_depth = jax.random.uniform(key_rows[6], (4,), minval=math.log(0.5), maxval=math.log(0.8))
    segment_runs = jnp.zeros((PACKED_TOKENS,), jnp.float32).at[segment_location].add(segment_depth)
    value_rows = -head_decay_rate[:, None] * shard_complete * token_multiplier + segment_runs[None, :]
    return value_rows.astype(jnp.float32)


def block_levels(own_key, extent, cuts, low, largest):
    gain = 1.0
    for position, blocks in cuts:
        steps = jax.random.uniform(jax.random.fold_in(jax.random.fold_in(own_key, 6), position), (blocks,), jnp.float32, low / len(cuts), largest / len(cuts))
        gain = gain * jnp.repeat(jnp.exp(steps), extent[position] // blocks).reshape((-1,) + (1,) * (len(extent) - 1 - position))
    return gain


def profile(count, total, bound, lean):
    weights = [(1 << 20) // math.isqrt(standing ** lean) + 1 for standing in range(2, count + 1)]
    surplus, holding = total - bound - (count - 1), [1] * (count - 1)
    while surplus > 0:
        free = [i for i in range(count - 1) if holding[i] < bound]
        mass, remaining = sum([weights[i] for i in free]), surplus
        for i in free:
            extra = min(bound - holding[i], max(1, remaining * weights[i] // mass), surplus)
            holding[i] = holding[i] + extra
            surplus = surplus - extra
    return np.array([bound] + holding)


def ragged_sizes(stream_key, number_of, total, most, slope):
    if number_of == 2:
        one = jax.random.randint(stream_key, (), max(1, total - most), min(most, total - 1) + 1)
        return jnp.stack([one, total - one])
    tallies = jnp.asarray(profile(number_of, total, most, slope), jnp.int32)
    twos = (number_of - 1) // 2
    donor, receiver = tallies[1:1 + 2 * twos:2], tallies[2:2 + 2 * twos:2]
    margin = jnp.minimum(donor - 1, most - receiver)
    passed = jax.random.randint(jax.random.fold_in(stream_key, 1), (twos,), 0, 1 << 20) % (margin + 1)
    tallies = tallies.at[1:1 + 2 * twos:2].set(donor - passed).at[2:2 + 2 * twos:2].set(receiver + passed)
    return tallies[jax.random.permutation(jax.random.fold_in(stream_key, 2), number_of)]


def normal_values(stream_key, extent, width, most, cuts=(), held_as=jnp.bfloat16):
    result = width * jax.random.normal(stream_key, extent, jnp.float32)
    if cuts:
        result = result * block_levels(stream_key, extent, cuts, -0.22, 0.18)
    return jnp.clip(result, -most, most).astype(held_as)


def setup_inputs(seed: int = 0) -> dict:
    key_of = jax.random.split(jax.random.key(seed), 10)
    return {
        "inputs": normal_values(key_of[0], (PACKED_TOKENS, H * P_SIZE), 0.1, 0.59765625, ((0, 8), (1, 4))),
        "gates": normal_values(key_of[1], (PACKED_TOKENS, H * P_SIZE), 1.0, 6.0, ((0, 8), (1, 4))),
        "write_keys": normal_values(key_of[2], (PACKED_TOKENS, N), 1.0, 6.0, ((0, 8),)),
        "read_keys": normal_values(key_of[3], (PACKED_TOKENS, N), (16 * N) ** -0.5, 0.125, ((0, 8),)),
        "log_decay": draw_log_decay(jax.random.fold_in(key_of[9], 71), 0),
        "skip_gain": jnp.clip(jnp.exp(math.log(4.0) - 2.0794415 * jax.random.uniform(key_of[5], (H,), jnp.float32) ** block_levels(key_of[5], (H,), ((0, 4),), -0.2, 0.2)), 0.5, 4.0),
        "doc_ids": jnp.searchsorted(jnp.cumsum(ragged_sizes(key_of[6], DOCS, PACKED_TOKENS, PACKED_TOKENS // 2, 0)), jnp.arange(PACKED_TOKENS), side="right").astype(jnp.int32),
        "out_weight": normal_values(key_of[7], (H * P_SIZE, D), (H * P_SIZE) ** -0.5, 0.078125, ((0, 4),)),
        "grad_out": normal_values(key_of[8], (PACKED_TOKENS, D), 1.0, 6.0, ((0, 32),)),
    }


def group_terms(write_blk, read_blk, decay_blk, doc_blk, before):
    block_len = doc_blk.shape[0]
    cumul = jnp.cumsum(decay_blk, axis=1)
    positions = jnp.arange(block_len)
    causal_same = (doc_blk[:, None] == doc_blk[None, :]) & (positions[:, None] >= positions[None, :])
    spread = jnp.where(causal_same[None], cumul[:, :, None] - cumul[:, None, :], 0.0)
    decay_matrix = jnp.where(causal_same[None], jnp.exp(spread), 0.0)
    scores = jnp.dot(read_blk, write_blk.T, preferred_element_type=jnp.float32)
    weights = (decay_matrix * scores[None]).astype(jnp.bfloat16)
    entry_w = jnp.where((doc_blk == before)[None], jnp.exp(cumul), 0.0)
    exit_w = jnp.where((doc_blk == doc_blk[block_len - 1])[None], jnp.exp(cumul[:, block_len - 1:] - cumul), 0.0)
    return weights, entry_w, exit_w, entry_w[:, block_len - 1]


def reference(inputs, gates, write_keys, read_keys, log_decay, skip_gain, doc_ids, out_weight, grad_out):
    tok_total, inner = inputs.shape
    head_count = log_decay.shape[0]
    head_width = inner // head_count
    state_width = write_keys.shape[1]
    group_count = tok_total // GROUP
    blocks_x = inputs.reshape(group_count, GROUP, head_count, head_width)
    blocks_b = write_keys.reshape(group_count, GROUP, state_width)
    blocks_c = read_keys.reshape(group_count, GROUP, state_width)
    blocks_d = log_decay.reshape(head_count, group_count, GROUP).transpose(1, 0, 2)
    doc_blocks = doc_ids.reshape(group_count, GROUP)
    befores = jnp.concatenate([jnp.full((1,), -1, jnp.int32), doc_blocks[:-1, GROUP - 1]])
    silu_gate = jax.nn.silu(gates.astype(jnp.float32))
    gate_blocks = silu_gate.reshape(group_count, GROUP, head_count, head_width)
    skip_full = skip_gain[None, :, None]
    empty_state = jnp.zeros((head_count, head_width, state_width), jnp.float32)

    def forward(entering, blk):
        x_blk, write_blk, read_blk, decay_blk, doc_blk, before, gate_blk = blk
        weights, entry_w, exit_w, block_decay = group_terms(write_blk, read_blk, decay_blk, doc_blk, before)
        inner_part = jnp.einsum('hts,shp->thp', weights.astype(jnp.float32), x_blk.astype(jnp.float32))
        rounded = lax.optimization_barrier(entering.astype(jnp.bfloat16)).astype(jnp.float32)
        carried = jnp.einsum('tn,hpn->thp', read_blk.astype(jnp.float32), rounded) * entry_w.T[:, :, None]
        mixed = inner_part + carried + skip_full * x_blk.astype(jnp.float32)
        gated = (mixed * gate_blk).astype(jnp.bfloat16)
        write_scaled = (exit_w.T[:, :, None] * x_blk.astype(jnp.float32)).astype(jnp.bfloat16)
        own_state = jnp.einsum('shp,sn->hpn', write_scaled.astype(jnp.float32), write_blk.astype(jnp.float32))
        return block_decay[:, None, None] * entering + own_state, gated

    _, gated_blocks = lax.scan(forward, empty_state, (blocks_x, blocks_b, blocks_c, blocks_d, doc_blocks, befores, gate_blocks))
    gated_all = gated_blocks.reshape(tok_total, inner)
    mixed_out = jnp.dot(gated_all, out_weight, preferred_element_type=jnp.float32).astype(jnp.bfloat16)

    grad_gated = jnp.dot(grad_out, out_weight.T, preferred_element_type=jnp.float32)
    grad_mix = (grad_gated * silu_gate).astype(jnp.bfloat16)
    blocks_dy = grad_mix.reshape(group_count, GROUP, head_count, head_width)

    def backward(arriving, blk):
        dy_blk, write_blk, read_blk, decay_blk, doc_blk, before = blk
        weights, entry_w, exit_w, block_decay = group_terms(write_blk, read_blk, decay_blk, doc_blk, before)
        inner_part = jnp.einsum('hts,thp->shp', weights.astype(jnp.float32), dy_blk.astype(jnp.float32))
        rounded = lax.optimization_barrier(arriving.astype(jnp.bfloat16)).astype(jnp.float32)
        carried = jnp.einsum('sn,hpn->shp', write_blk.astype(jnp.float32), rounded) * exit_w.T[:, :, None]
        grad_blk = (inner_part + carried + skip_full * dy_blk.astype(jnp.float32)).astype(jnp.bfloat16)
        grad_scaled = (entry_w.T[:, :, None] * dy_blk.astype(jnp.float32)).astype(jnp.bfloat16)
        own_state = jnp.einsum('thp,tn->hpn', grad_scaled.astype(jnp.float32), read_blk.astype(jnp.float32))
        return own_state + block_decay[:, None, None] * arriving, grad_blk

    _, grad_blocks = lax.scan(backward, empty_state, (blocks_dy, blocks_b, blocks_c, blocks_d, doc_blocks, befores), reverse=True)
    return mixed_out, grad_blocks.reshape(tok_total, inner)
```

```python
import functools
import math

import jax
import jax.numpy as jnp
from jax import lax
from jax.experimental import pallas as pl
from jax.experimental.pallas import tpu as pltpu
from jax.sharding import PartitionSpec as P

GROUP = 256
LANES = 128
LOG2E = math.log2(math.e)
F32 = jnp.float32
BF16 = jnp.bfloat16
NT = (((1,), (1,)), ((), ()))
TN = (((0,), (0,)), ((), ()))
VMEM_LIMIT = 56 * 2**20


def dot(a, b, dims=(((1,), (0,)), ((), ()))):
    return lax.dot_general(a, b, dims, preferred_element_type=F32)


def params():
    return pltpu.CompilerParams(vmem_limit_bytes=VMEM_LIMIT)


def cost(flops, nbytes):
    return pl.CostEstimate(flops=int(flops), bytes_accessed=int(nbytes), transcendentals=0)


def lanes_exact(row, spread):
    high = row.astype(BF16)
    low = (row - high.astype(F32)).astype(BF16)
    return dot(high, spread) + dot(low, spread)


def silu(gates):
    v = gates.astype(F32)
    return v / (1.0 + jnp.exp(-v))


def state_kernel(
    heads, place, x_ref, b_ref, ld_ref, doc_ref, spread_ref,
    ccol_ref, crow_ref, local_ref, keep_ref, send_ref, pre_ref, blk_ref,
    padded, running, total, last_doc,
):
    k = pl.program_id(0)
    half = running.shape[0] // 2

    @pl.when(k == 0)
    def _():
        padded[...] = jnp.zeros_like(padded)
        running[...] = jnp.zeros_like(running)
        total[...] = jnp.zeros_like(total)
        last_doc[...] = jnp.zeros_like(last_doc)
        pre_ref[...] = jnp.zeros_like(pre_ref)
        blk_ref[...] = jnp.zeros_like(blk_ref)

    padded[0:heads, :] = ld_ref[...]
    upto = lax.broadcasted_iota(jnp.int32, (GROUP, GROUP), 1) <= lax.broadcasted_iota(
        jnp.int32, (GROUP, GROUP), 0
    )
    cum = lax.dot_general(
        padded[...], upto.astype(F32), NT, precision=lax.Precision.HIGHEST,
        preferred_element_type=F32,
    ) * LOG2E
    rows = lax.broadcasted_iota(jnp.int32, (LANES, GROUP), 0)
    cum = jnp.where(rows == LANES - 1, doc_ref[...].astype(F32), cum)
    crow_ref[...] = cum[0 : crow_ref.shape[0]]
    ccol = cum.T
    ccol_ref[...] = ccol
    docs = ccol[:, LANES - 1 :]
    end = ccol[GROUP - 1 :]
    end_doc = end[:, LANES - 1 :]
    exit_w = jnp.where(docs == end_doc, jnp.exp2(jnp.minimum(end - ccol, 0.0)), 0.0).astype(BF16)
    spread = spread_ref[...]
    scaled = (dot(exit_w, spread) * x_ref[...].astype(F32)).astype(BF16)
    own = dot(b_ref[...], scaled, TN)
    same = end_doc == last_doc[0:1, 0:1]
    block_decay = jnp.where(same, jnp.exp2(end), 0.0)
    prefix = jnp.exp2(total[0:1])
    stacked = jnp.concatenate(
        [block_decay, prefix, jnp.exp2(total[0:1] + end), jnp.zeros((5, LANES), F32)], axis=0
    )
    wide = lanes_exact(stacked, spread)
    sub = lax.broadcasted_iota(jnp.int32, blk_ref.shape, 0)
    blk_ref[...] = jnp.where(sub == k, wide[0:1], blk_ref[...])
    pre_ref[...] = jnp.where(
        sub == k, wide[1:2], jnp.where(sub == k + 1, wide[2:3], pre_ref[...])
    )
    local_ref[0] = running[...].astype(BF16)
    running[...] = wide[0:1] * running[...] + own
    total[...] = total[...] + end
    last_doc[...] = jnp.broadcast_to(end_doc, last_doc.shape)

    @pl.when(k == pl.num_programs(0) - 1)
    def _():
        at = place[0]
        keep_ref[...] = running[pl.ds(at * half, half), :].astype(BF16)
        send_ref[...] = running[pl.ds((1 - at) * half, half), :].astype(BF16)


def local_states(inputs, write_keys, log_decay, docs_row, spread, side):
    tokens, inner = inputs.shape
    heads = log_decay.shape[0]
    n = write_keys.shape[1]
    blocks = tokens // GROUP
    head_rows = -(-heads // 8) * 8
    pre_rows = -(-(blocks + 1) // 8) * 8
    return pl.pallas_call(
        lambda place, *refs: state_kernel(heads, place, *refs),
        grid_spec=pltpu.PrefetchScalarGridSpec(
            num_scalar_prefetch=1,
            grid=(blocks,),
            in_specs=[
                pl.BlockSpec((GROUP, inner), lambda k, s: (k, 0)),
                pl.BlockSpec((GROUP, n), lambda k, s: (k, 0)),
                pl.BlockSpec((heads, GROUP), lambda k, s: (0, k)),
                pl.BlockSpec((1, GROUP), lambda k, s: (0, k)),
                pl.BlockSpec((LANES, inner), lambda k, s: (0, 0)),
            ],
            out_specs=[
                pl.BlockSpec((GROUP, LANES), lambda k, s: (k, 0)),
                pl.BlockSpec((head_rows, GROUP), lambda k, s: (0, k)),
                pl.BlockSpec((1, n, inner), lambda k, s: (k, 0, 0)),
                pl.BlockSpec((n // 2, inner), lambda k, s: (0, 0)),
                pl.BlockSpec((n // 2, inner), lambda k, s: (0, 0)),
                pl.BlockSpec((pre_rows, inner), lambda k, s: (0, 0)),
                pl.BlockSpec((pre_rows, inner), lambda k, s: (0, 0)),
            ],
            scratch_shapes=[
                pltpu.VMEM((LANES, GROUP), F32),
                pltpu.VMEM((n, inner), F32),
                pltpu.VMEM((8, LANES), F32),
                pltpu.VMEM((8, LANES), F32),
            ],
        ),
        out_shape=[
            jax.ShapeDtypeStruct((tokens, LANES), F32),
            jax.ShapeDtypeStruct((head_rows, tokens), F32),
            jax.ShapeDtypeStruct((blocks, n, inner), BF16),
            jax.ShapeDtypeStruct((n // 2, inner), BF16),
            jax.ShapeDtypeStruct((n // 2, inner), BF16),
            jax.ShapeDtypeStruct((pre_rows, inner), F32),
            jax.ShapeDtypeStruct((pre_rows, inner), F32),
        ],
        compiler_params=params(),
        cost_estimate=cost(4 * tokens * inner * n, tokens * inner * 2 * 3),
        name="local_states",
    )(side, inputs, write_keys, log_decay, docs_row, spread)


def inside_kernel(
    heads, width, backward, x_ref, b_ref, c_ref, ccol_ref, crow_ref, doc_ref, skip_ref, out_ref
):
    half = GROUP // 2
    col = ccol_ref[...]
    docs_col = col[:, LANES - 1 :]
    docs_row = doc_ref[...].astype(F32)
    rows = lax.broadcasted_iota(jnp.int32, (GROUP, GROUP), 0)
    cols = lax.broadcasted_iota(jnp.int32, (GROUP, GROUP), 1)
    if backward:
        scores = dot(b_ref[...], c_ref[...], NT)
        allowed = (docs_col == docs_row) & (rows <= cols)
    else:
        scores = dot(c_ref[...], b_ref[...], NT)
        allowed = (docs_col == docs_row) & (cols <= rows)
    scores = jnp.where(allowed, scores, 0.0)
    lane = lax.broadcasted_iota(jnp.int32, (GROUP, LANES), 1)
    per = LANES // width
    for j in range(heads // per):
        cut = slice(j * LANES, (j + 1) * LANES)
        x = x_ref[:, cut]
        base = skip_ref[:, cut] * x.astype(F32)
        top, bottom = base[:half], base[half:]
        for i in range(per):
            h = j * per + i
            own = jnp.where(lane // width == i, x, jnp.zeros_like(x))
            at_row = crow_ref[h : h + 1, :]
            at_col = col[:, h : h + 1]

            def weights(r, c):
                if backward:
                    gap = at_row[:, c] - at_col[r]
                else:
                    gap = at_col[r] - at_row[:, c]
                return (jnp.exp2(jnp.minimum(gap, 0.0)) * scores[r, c]).astype(BF16)

            low, high, both = slice(0, half), slice(half, GROUP), slice(0, GROUP)
            if backward:
                top = top + dot(weights(low, both), own)
                bottom = bottom + dot(weights(high, high), own[half:])
            else:
                top = top + dot(weights(low, low), own[:half])
                bottom = bottom + dot(weights(high, both), own)
        out_ref[:half, cut] = top.astype(BF16)
        out_ref[half:, cut] = bottom.astype(BF16)


def inside(x, write_keys, read_keys, ccol, crow, docs_row, skip, heads, backward):
    tokens, inner = x.shape
    n = write_keys.shape[1]
    head_rows = crow.shape[0]
    return pl.pallas_call(
        functools.partial(inside_kernel, heads, inner // heads, backward),
        grid=(tokens // GROUP,),
        in_specs=[
            pl.BlockSpec((GROUP, inner), lambda k: (k, 0)),
            pl.BlockSpec((GROUP, n), lambda k: (k, 0)),
            pl.BlockSpec((GROUP, n), lambda k: (k, 0)),
            pl.BlockSpec((GROUP, LANES), lambda k: (k, 0)),
            pl.BlockSpec((head_rows, GROUP), lambda k: (0, k)),
            pl.BlockSpec((1, GROUP), lambda k: (0, k)),
            pl.BlockSpec((1, inner), lambda k: (0, 0)),
        ],
        out_specs=pl.BlockSpec((GROUP, inner), lambda k: (k, 0)),
        out_shape=jax.ShapeDtypeStruct((tokens, inner), BF16),
        compiler_params=params(),
        cost_estimate=cost(8 * tokens * inner * GROUP, tokens * inner * 4),
        name="inside_backward" if backward else "inside_forward",
    )(x, write_keys, read_keys, ccol, crow, docs_row, skip)


def entry_wide(ccol, prior, spread):
    docs = ccol[:, LANES - 1 :]
    entry = jnp.where(docs == prior, jnp.exp2(ccol), 0.0).astype(BF16)
    return dot(entry, spread)


def tail_kernel(count, chunk, blocks, scalars, *refs):
    (mixed_refs, gate_refs, read_refs, ccol_refs, local_refs), rest = (
        [refs[i * count : (i + 1) * count] for i in range(5)],
        refs[5 * count :],
    )
    keep_ref, other_ref, pre_ref, spread_ref, w_ref = rest[:5]
    outs, gated = rest[5 : 5 + count], rest[5 + count]
    half = keep_ref.shape[0]

    @pl.when(pl.program_id(0) == 0)
    def _():
        before, side = scalars[0], scalars[1]
        at_low = side == 0
        keep, other = keep_ref[...].astype(F32), other_ref[...].astype(F32)
        state = jnp.concatenate(
            [jnp.where(at_low, keep, other), jnp.where(at_low, other, keep)], axis=0
        )
        sub = lax.broadcasted_iota(jnp.int32, pre_ref.shape, 0)
        for i in range(count):
            k = scalars[2 + blocks + i] * chunk // GROUP
            prior = jnp.where(k == 0, before, scalars[1 + jnp.maximum(k, 1)])
            live = (prior == before).astype(F32)
            decay = jnp.sum(jnp.where(sub == k, pre_ref[...], 0.0), axis=0, keepdims=True) * live
            entering = (local_refs[i][0].astype(F32) + decay * state).astype(BF16)
            carried = dot(read_refs[i][...], entering) * entry_wide(
                ccol_refs[i][...], prior.astype(F32), spread_ref[...]
            )
            gated[i] = (
                (mixed_refs[i][...].astype(F32) + carried) * silu(gate_refs[i][...])
            ).astype(BF16)

    for i in range(count):
        outs[i][...] = dot(gated[i], w_ref[...]).astype(BF16)


def forward_tail(
    chunk, scalars, count, mixed, gates, read_keys, ccol, local, keep, other, pre, spread, out_weight
):
    inner, width = out_weight.shape
    n = read_keys.shape[1]
    blocks = local.shape[0]
    tile = 512 if width % 512 == 0 else width
    pick = lambda i: (lambda j, s: (s[2 + blocks + i], 0))
    fixed = lambda shape: pl.BlockSpec(shape, lambda j, s: (0, 0))
    each = lambda shape: [pl.BlockSpec(shape, pick(i)) for i in range(count)]
    in_specs = (
        each((chunk, inner)) + each((chunk, inner)) + each((chunk, n)) + each((chunk, LANES))
        + [
            pl.BlockSpec(
                (1, n, inner), lambda j, s, i=i: (s[2 + blocks + i] * chunk // GROUP, 0, 0)
            )
            for i in range(count)
        ]
        + [
            fixed(keep.shape), fixed(other.shape), fixed(pre.shape), fixed(spread.shape),
            pl.BlockSpec((inner, tile), lambda j, s: (0, j)),
        ]
    )
    return pl.pallas_call(
        functools.partial(tail_kernel, count, chunk, blocks),
        grid_spec=pltpu.PrefetchScalarGridSpec(
            num_scalar_prefetch=1,
            grid=(width // tile,),
            in_specs=in_specs,
            out_specs=[pl.BlockSpec((chunk, tile), lambda j, s: (0, j))] * count,
            scratch_shapes=[pltpu.VMEM((count, chunk, inner), BF16)],
        ),
        out_shape=[jax.ShapeDtypeStruct((chunk, width), BF16)] * count,
        compiler_params=params(),
        cost_estimate=cost(
            2 * count * chunk * inner * width, inner * width * 2 + count * chunk * (inner * 4 + width * 2)
        ),
        name="forward_tail",
    )(
        scalars, *[mixed] * count, *[gates] * count, *[read_keys] * count, *[ccol] * count,
        *[local] * count, keep, other, pre, spread, out_weight,
    )


def grad_kernel(count, chunk, blocks, first, final, scalars, *refs):
    go_refs, gate_refs, read_refs, ccol_refs = [refs[i * count : (i + 1) * count] for i in range(4)]
    rest = list(refs[4 * count :])
    pre_ref, spread_ref, w_ref = rest[:3]
    rest = rest[3:]
    if not first:
        sum_in, rest = rest[0], rest[1:]
    mix_refs, state_refs, rest = rest[:count], rest[count : 2 * count], rest[2 * count :]
    before, side = scalars[0], scalars[1]
    sub = lax.broadcasted_iota(jnp.int32, pre_ref.shape, 0)
    summed = None if first else sum_in[...]
    for i in range(count):
        k = scalars[2 + blocks + i] * chunk // GROUP
        prior = jnp.where(k == 0, before, scalars[1 + jnp.maximum(k, 1)])
        live = (prior == before).astype(F32)
        mix = (dot(go_refs[i][...], w_ref[...], NT) * silu(gate_refs[i][...])).astype(BF16)
        mix_refs[i][...] = mix
        scaled = (
            entry_wide(ccol_refs[i][...], prior.astype(F32), spread_ref[...]) * mix.astype(F32)
        ).astype(BF16)
        state = dot(read_refs[i][...], scaled, TN)
        state_refs[i][...] = state.astype(BF16)
        decay = jnp.sum(jnp.where(sub == k, pre_ref[...], 0.0), axis=0, keepdims=True) * live
        part = decay * state
        summed = part if summed is None else summed + part
    if final:
        half = summed.shape[0] // 2
        at_low = side == 0
        rest[0][...] = jnp.where(at_low, summed[:half], summed[half:]).astype(BF16)
        rest[1][...] = jnp.where(at_low, summed[half:], summed[:half]).astype(BF16)
    else:
        rest[0][...] = summed


def grad_chunks(
    chunk, scalars, blocks, arrived, gates, read_keys, ccol, pre, spread, out_weight, summed, final
):
    count = len(arrived)
    inner, width = out_weight.shape
    n = read_keys.shape[1]
    tile = 256 if inner % 256 == 0 else LANES
    first = summed is None
    tiled = lambda rows: pl.BlockSpec((rows, tile), lambda j, s: (0, j))
    in_specs = (
        [pl.BlockSpec((chunk, width), lambda j, s: (0, 0))] * count
        + [pl.BlockSpec((chunk, tile), lambda j, s, i=i: (s[2 + blocks + i], j)) for i in range(count)]
        + [pl.BlockSpec((chunk, n), lambda j, s, i=i: (s[2 + blocks + i], 0)) for i in range(count)]
        + [pl.BlockSpec((chunk, LANES), lambda j, s, i=i: (s[2 + blocks + i], 0)) for i in range(count)]
        + [tiled(pre.shape[0]), tiled(LANES), pl.BlockSpec((tile, width), lambda j, s: (j, 0))]
        + ([] if first else [tiled(n)])
    )
    out_shape = [jax.ShapeDtypeStruct((chunk, inner), BF16)] * count + [
        jax.ShapeDtypeStruct((n, inner), BF16)
    ] * count
    out_specs = [tiled(chunk)] * count + [tiled(n)] * count
    if final:
        out_shape += [jax.ShapeDtypeStruct((n // 2, inner), BF16)] * 2
        out_specs += [tiled(n // 2)] * 2
    else:
        out_shape += [jax.ShapeDtypeStruct((n, inner), F32)]
        out_specs += [tiled(n)]
    res = pl.pallas_call(
        functools.partial(grad_kernel, count, chunk, blocks, first, final),
        grid_spec=pltpu.PrefetchScalarGridSpec(
            num_scalar_prefetch=1, grid=(inner // tile,), in_specs=in_specs, out_specs=out_specs
        ),
        out_shape=out_shape,
        compiler_params=params(),
        cost_estimate=cost(
            2 * count * chunk * inner * width, inner * width * 2 + count * chunk * (inner * 4 + width * 2)
        ),
        name="grad_chunks",
    )(
        scalars, *arrived, *[gates] * count, *[read_keys] * count, *[ccol] * count,
        pre, spread, out_weight, *([] if first else [summed]),
    )
    return res[:count], res[count : 2 * count], res[2 * count :]


def back_kernel(per, place, part_ref, b_ref, ccol_ref, state_ref, blk_ref, keep_ref, other_ref,
                spread_ref, out_ref, running):
    step = pl.program_id(0)
    k = pl.num_programs(0) - 1 - step
    half = keep_ref.shape[0]

    @pl.when(step == 0)
    def _():
        at = place[0]
        running[pl.ds(at * half, half), :] = keep_ref[...].astype(F32)
        running[pl.ds((1 - at) * half, half), :] = other_ref[...].astype(F32)

    ccol = ccol_ref[...]
    end = ccol[GROUP - 1 :]
    docs = ccol[:, LANES - 1 :]
    exit_w = jnp.where(
        docs == end[:, LANES - 1 :], jnp.exp2(jnp.minimum(end - ccol, 0.0)), 0.0
    ).astype(BF16)
    carried = dot(b_ref[...], running[...].astype(BF16)) * dot(exit_w, spread_ref[...])
    out_ref[...] = (part_ref[...].astype(F32) + carried).astype(BF16)
    sub = lax.broadcasted_iota(jnp.int32, blk_ref.shape, 0)
    decay = jnp.sum(jnp.where(sub == k, blk_ref[...], 0.0), axis=0, keepdims=True)
    state = state_ref[0].astype(F32)
    for i in range(1, per):
        state = state + state_ref[i].astype(F32)
    running[...] = state + decay * running[...]


def back_tail(side, part, write_keys, ccol, states, blk, keep, other, spread):
    tokens, inner = part.shape
    n = write_keys.shape[1]
    blocks = tokens // GROUP
    per = states.shape[0] // blocks
    turn = lambda j, s: (blocks - 1 - j, 0)
    fixed = lambda shape: pl.BlockSpec(shape, lambda j, s: (0, 0))
    return pl.pallas_call(
        functools.partial(back_kernel, per),
        grid_spec=pltpu.PrefetchScalarGridSpec(
            num_scalar_prefetch=1,
            grid=(blocks,),
            in_specs=[
                pl.BlockSpec((GROUP, inner), turn),
                pl.BlockSpec((GROUP, n), turn),
                pl.BlockSpec((GROUP, LANES), turn),
                pl.BlockSpec((per, n, inner), lambda j, s: (blocks - 1 - j, 0, 0)),
                fixed(blk.shape), fixed(keep.shape), fixed(other.shape), fixed(spread.shape),
            ],
            out_specs=pl.BlockSpec((GROUP, inner), turn),
            scratch_shapes=[pltpu.VMEM((n, inner), F32)],
        ),
        out_shape=jax.ShapeDtypeStruct((tokens, inner), BF16),
        compiler_params=params(),
        cost_estimate=cost(2 * tokens * inner * n, tokens * inner * 4),
        name="back_tail",
    )(side, part, write_keys, ccol, states, blk, keep, other, spread)


def shifted(block, axis, distance):
    size = lax.axis_size(axis)
    route = [(i, i + distance) for i in range(size) if 0 <= i + distance < size]
    return lax.ppermute(block, axis, route)


def swapped(block, axis):
    return lax.ppermute(block, axis, [(i, i ^ 1) for i in range(lax.axis_size(axis))])


def rotated(block, axis, distance):
    size = lax.axis_size(axis)
    return lax.ppermute(block, axis, [(i, (i + distance) % size) for i in range(size)])


def scan_shards(keep, send, own_decay, mate_decay, first_in_pair, way):
    size = lax.axis_size("seq")
    window = max(size // 4, 1)
    keep_f = keep.astype(F32)
    got = swapped(send, "seq").astype(F32)
    near = jnp.where(first_in_pair, keep_f, got)
    far = jnp.where(first_in_pair, got, keep_f)
    near_decay = jnp.where(first_in_pair, own_decay, mate_decay)
    far_decay = jnp.where(first_in_pair, mate_decay, own_decay)
    total = (far + far_decay * near).astype(BF16)
    decay = own_decay * mate_decay
    reach = 1
    while reach < window:
        total = (total.astype(F32) + decay * shifted(total, "seq", 2 * way * reach).astype(F32)).astype(
            BF16
        )
        if 2 * reach < window:
            decay = decay * shifted(decay, "seq", 2 * way * reach)
        reach *= 2
    at_first = shifted(total, "seq", 2 * way).astype(F32)
    at_second = near + near_decay * at_first
    mine = jnp.where(first_in_pair, at_first, at_second).astype(BF16)
    hers = jnp.where(first_in_pair, at_second, at_first).astype(BF16)
    return mine, swapped(hers, "seq")


def shards(
    inputs, gates, write_keys, read_keys, log_decay, skip_gain, doc_ids, out_weight, grad_out
):
    tokens, inner = inputs.shape
    heads = log_decay.shape[0]
    width = inner // heads
    blocks = tokens // GROUP
    members = lax.axis_size("head")
    chips = members // 2
    chunk = tokens // members
    here = lax.axis_index("head")
    chip, core = here // 2, here % 2
    side = (lax.axis_index("seq") % 2).astype(jnp.int32)
    low = side == 0

    sibling = swapped(grad_out, "head")
    remote = [rotated(grad_out, "head", 2 * d) for d in range(1, chips)]
    relayed = [swapped(part, "head") for part in remote]

    ends = doc_ids[GROUP - 1 :: GROUP]
    last = doc_ids[tokens - 1 :] + 1
    before1 = shifted(last, "seq", 1)
    before2 = shifted(last, "seq", 2)
    mate_last = swapped(last, "seq")
    own_same = (last == before1).astype(F32)
    mate_same = jnp.where(low, mate_last == last, mate_last == before2).astype(F32)
    base = jnp.concatenate([before1 - 1, side[None], ends])

    spread = (
        jnp.arange(LANES)[:, None] == (jnp.arange(inner) // width)[None, :]
    ).astype(BF16)
    docs_row = doc_ids[None, :]
    skip = jnp.repeat(skip_gain, width)[None, :]

    ccol, crow, local, keep, send, pre, blk = local_states(
        inputs, write_keys, log_decay, docs_row, spread, side[None]
    )
    own_raw = pre[blocks : blocks + 1]
    own_decay = own_raw * own_same
    mate_decay = swapped(own_raw, "seq") * mate_same
    enter_keep, enter_other = scan_shards(keep, send, own_decay, mate_decay, low, 1)

    mixed = inside(inputs, write_keys, read_keys, ccol, crow, docs_row, skip, heads, False)

    numbers = lambda *qs: jnp.concatenate([base, jnp.stack(qs).astype(jnp.int32)])
    args = (gates, read_keys, ccol, pre, spread, out_weight)
    mate = here ^ 1
    q_remote = [(here - 2 * d) % members for d in range(1, chips)]
    q_relayed = [q ^ 1 for q in q_remote]
    groups = [([here, mate], [grad_out, sibling])]
    for d in range(chips - 1):
        groups.append(([q_remote[d]], [remote[d]]))
        groups.append(([q_relayed[d]], [relayed[d]]))
    summed, order, mixes, states = None, [], [], []
    for at, (qs, arrived) in enumerate(groups):
        final = at == len(groups) - 1
        mix, state, rest = grad_chunks(
            chunk, numbers(*qs), blocks, arrived, *args, summed, final
        )
        order += qs
        mixes += mix
        states += state
        summed = rest[0]
    back_keep, back_send = rest
    arrive_keep, arrive_other = scan_shards(
        back_keep, back_send, own_decay, mate_decay, jnp.logical_not(low), -1
    )

    tail = lambda *qs: forward_tail(
        chunk, numbers(*qs), len(qs), mixed, gates, read_keys, ccol, local,
        enter_keep, enter_other, pre, spread, out_weight,
    )
    landed = []
    for d in range(1, chips):
        target = ((chip + d) % chips) * 2
        give, stay = tail(target + 1 - core, target + core)
        both = (stay.astype(F32) + swapped(give, "head").astype(F32)).astype(BF16)
        landed.append(rotated(both, "head", 2 * d))
    give, stay = tail(mate, here)
    out = stay.astype(F32) + swapped(give, "head").astype(F32)
    for part in landed:
        out = out + part.astype(F32)
    mixed_out = out.astype(BF16)

    slot = jnp.zeros((members,), jnp.int32).at[jnp.stack(order)].set(jnp.arange(members, dtype=jnp.int32))
    mix_all = jnp.stack(mixes)[slot].reshape(tokens, inner)
    state_all = jnp.stack(states)[slot]
    part = inside(mix_all, write_keys, read_keys, ccol, crow, docs_row, skip, heads, True)
    grad_inputs = back_tail(
        side[None], part, write_keys, ccol, state_all, blk, arrive_keep, arrive_other, spread
    )
    return mixed_out, grad_inputs


def solution(mesh):
    in_specs = (
        P("seq", "head"),
        P("seq", "head"),
        P("seq", None),
        P("seq", None),
        P("head", "seq"),
        P("head"),
        P("seq"),
        P("head", None),
        P(("seq", "head"), None),
    )
    out_specs = (P(("seq", "head"), None), P("seq", "head"))
    return jax.shard_map(shards, mesh=mesh, in_specs=in_specs, out_specs=out_specs, check_vma=False)
```

```python
import functools
import math

import jax
import jax.numpy as jnp
from jax import lax
from jax.experimental import pallas as pl
from jax.experimental.pallas import tpu as pltpu
from jax.sharding import PartitionSpec as P

GROUP = 256
LANES = 128
TILE = 16
LOG2E = math.log2(math.e)
F32 = jnp.float32
BF16 = jnp.bfloat16
NT = (((1,), (1,)), ((), ()))
TN = (((0,), (0,)), ((), ()))
VM = pl.BlockSpec(memory_space=pltpu.VMEM)
SM = pl.BlockSpec(memory_space=pltpu.SMEM)
HB = pl.BlockSpec(memory_space=pltpu.HBM)
DECAY, DECAY_REST, LAST, FIRST = range(4)


def dot(a, b, dims=(((1,), (0,)), ((), ()))):
    return lax.dot_general(a, b, dims, preferred_element_type=F32)


def call(kernel, name, out_shape, in_specs, args, limit_mib=16, scratch=(), aliases=None):
    space = {id(VM): pltpu.VMEM, id(HB): pltpu.HBM}
    args = [
        arg if spec is SM else pltpu.with_memory_space_constraint(arg, space[id(spec)])
        for spec, arg in zip(in_specs, args, strict=True)
    ]
    return pl.pallas_call(
        kernel,
        in_specs=in_specs,
        out_specs=[VM if o.memory_space == pltpu.VMEM else HB for o in out_shape],
        out_shape=out_shape,
        scratch_shapes=scratch,
        input_output_aliases=aliases or {},
        compiler_params=pltpu.CompilerParams(vmem_limit_bytes=limit_mib * 2**20),
        cost_estimate=pl.CostEstimate(flops=1, bytes_accessed=1, transcendentals=0),
        name=name,
    )(*args)


def start(sems, *pairs):
    copies = [
        pltpu.make_async_copy(source, target, sems.at[i]) for i, (source, target) in enumerate(pairs)
    ]
    for copy in copies:
        copy.start()
    return copies


def split(value):
    high = value.astype(BF16)
    return high, (value - high.astype(F32)).astype(BF16)


def silu(gates):
    v = gates.astype(F32)
    return 0.5 * v * (1.0 + jnp.tanh(0.5 * v))


def row_at(rows, k):
    return jnp.sum(jnp.where(iota(rows.shape, 0) == k, rows, 0.0), axis=0, keepdims=True)


def iota(shape, dim):
    return lax.broadcasted_iota(jnp.int32, shape, dim)


def state_kernel(
    heads, blocks, places, x_hbm, b_hbm, c_hbm, ld_hbm, doc_ref, spread_ref,
    crow_ref, entry_ref, exit_ref, local_ref, keep_ref, send_ref, pre_ref, blk_ref, info_ref,
    x_ref, b_ref, c_ref, padded, running, ld_ref, sems,
):
    n, inner = running.shape
    half = n // 2
    parts = [pl.ds(k * GROUP, GROUP) for k in range(blocks)]
    ld_copy, b_copy, c_copy, *x_copies = start(
        sems, (ld_hbm, ld_ref), (b_hbm, b_ref), (c_hbm, c_ref),
        *[(x_hbm.at[p], x_ref.at[p]) for p in parts],
    )
    head_rows = crow_ref.shape[1]
    spread = spread_ref[...]
    later = (iota((GROUP, GROUP), 0) <= iota((GROUP, GROUP), 1)).astype(BF16)
    padded[...] = jnp.zeros_like(padded)
    row = iota((head_rows, GROUP), 0)
    pre_ref[...] = jnp.zeros_like(pre_ref)
    blk_ref[...] = jnp.zeros_like(blk_ref)
    info_ref[...] = jnp.zeros_like(info_ref)
    first_doc = last_doc = total = None
    ld_copy.wait()
    for k in range(blocks):
        at = slice(k * GROUP, (k + 1) * GROUP)
        padded[0:heads, :] = ld_ref[:, at] * LOG2E
        steps = padded[0:head_rows, :]
        high, rest = split(steps)
        mid, low = split(steps - high.astype(F32))
        cum = dot(high, later) + (dot(mid, later) + dot(low, later))
        cum = jnp.where(row == head_rows - 1, doc_ref[:, at].astype(F32), cum)
        crow_ref[k] = cum
        padded[0:head_rows, :] = cum
        ccol = padded[...].T
        padded[0:head_rows, :] = jnp.zeros((head_rows, GROUP), F32)
        docs = ccol[:, head_rows - 1 : head_rows]
        end = ccol[GROUP - 1 :]
        end_doc = end[:, head_rows - 1 : head_rows]
        if k == 0:
            first_doc = ccol[0:1, head_rows - 1 : head_rows]
            last_doc = first_doc
            total = jnp.zeros_like(end)
        exit_w = jnp.where(docs == end_doc, jnp.exp2(jnp.minimum(end - ccol, 0.0)), 0.0).astype(BF16)
        exit_ref[at, :] = exit_w
        entry_ref[at, :] = jnp.where(docs == last_doc, jnp.exp2(jnp.minimum(ccol, 0.0)), 0.0).astype(BF16)
        if k == 0:
            b_copy.wait()
        x_copies[k].wait()
        scaled = (dot(exit_w, spread) * x_ref[at, :].astype(F32)).astype(BF16)
        own = dot(b_ref[at, :], scaled, TN)
        block_decay = jnp.where(end_doc == last_doc, jnp.exp2(end), 0.0)
        whole = jnp.exp2(total + end)
        stacked = jnp.concatenate(
            [block_decay, jnp.where(end_doc == first_doc, whole, 0.0), whole, jnp.zeros((5, LANES), F32)],
            axis=0,
        )
        high, rest = split(stacked)
        wide = dot(high, spread) + dot(rest, spread)
        blk_ref[k : k + 1, :] = wide[0:1]
        if k == 0:
            local_ref[k] = jnp.zeros((n, inner), BF16)
            pre_ref[0:1, :] = jnp.ones((1, inner), F32)
            running[...] = own
        else:
            local_ref[k] = running[...].astype(BF16)
            running[...] = wide[0:1] * running[...] + own
        if k < blocks - 1:
            pre_ref[k + 1 : k + 2, :] = wide[1:2]
        total = total + end
        last_doc = end_doc
    raw = wide[2:3]
    last_row = jnp.broadcast_to(last_doc + 1.0, (1, inner))
    first_row = jnp.broadcast_to(first_doc + 1.0, (1, inner))
    info_ref[0:1, :] = raw
    info_ref[1:2, :] = last_row
    info_ref[2:3, :] = first_row
    side = places[0]
    keep_ref[...] = running[pl.ds(pl.multiple_of(side * half, half), half), :].astype(BF16)
    send_ref[0:half, :] = running[pl.ds(pl.multiple_of((1 - side) * half, half), half), :].astype(BF16)
    send_ref[half:, :] = tags(raw, last_row, first_row)
    c_copy.wait()


def tags(decay, last, first):
    high, rest = split(decay)
    rows = [high.astype(F32), rest.astype(F32), last, first]
    rows.append(jnp.zeros((TILE - len(rows), decay.shape[1]), F32))
    return jnp.concatenate(rows, axis=0).astype(BF16)


def untagged(block):
    half = block.shape[0] - TILE
    state, rows = block[:half].astype(F32), block[half:].astype(F32)
    row = lambda i: rows[i : i + 1]
    return state, row(DECAY) + row(DECAY_REST), row(LAST), row(FIRST)


def local_states(places, inputs, write_keys, read_keys, log_decay, docs_row, spread):
    tokens, inner = inputs.shape
    heads = log_decay.shape[0]
    n = write_keys.shape[1]
    blocks = tokens // GROUP
    head_rows = -(-(heads + 1) // 8) * 8
    block_rows = -(-blocks // 8) * 8
    return call(
        functools.partial(state_kernel, heads, blocks),
        "local_states",
        [
            pltpu.VMEM((blocks, head_rows, GROUP), F32),
            pltpu.VMEM((tokens, LANES), BF16),
            pltpu.VMEM((tokens, LANES), BF16),
            pltpu.VMEM((blocks, n, inner), BF16),
            pltpu.VMEM((n // 2, inner), BF16),
            pltpu.VMEM((n // 2 + TILE, inner), BF16),
            pltpu.VMEM((block_rows, inner), F32),
            pltpu.VMEM((block_rows, inner), F32),
            pltpu.VMEM((8, inner), F32),
            pltpu.VMEM((tokens, inner), BF16),
            pltpu.VMEM((tokens, n), BF16),
            pltpu.VMEM((tokens, n), BF16),
        ],
        [SM] + [HB] * 4 + [VM] * 2,
        (places, inputs, write_keys, read_keys, log_decay, docs_row, spread),
        scratch=[
            pltpu.VMEM((LANES, GROUP), F32),
            pltpu.VMEM((n, inner), F32),
            pltpu.VMEM((heads, tokens), F32),
            pltpu.SemaphoreType.DMA((3 + blocks,)),
        ],
    )


def inside_kernel(heads, width, blocks, backward, fetched, x_ref, b_ref, c_ref, crow_ref, skip_ref, _, *rest):
    fetch_hbm, out_ref, fetch_vm, padded = (
        rest[:fetched], rest[fetched], rest[fetched + 1 : 2 * fetched + 1], rest[2 * fetched + 1]
    )
    copies = start(rest[2 * fetched + 2], *zip(fetch_hbm, fetch_vm)) if fetched else []
    half = GROUP // 2
    head_rows = crow_ref.shape[1]
    per = LANES // width
    part = lambda k: pl.ds(pl.multiple_of(k * GROUP, GROUP), GROUP)
    lane = iota((GROUP, LANES), 1)
    rows, cols = iota((GROUP, GROUP), 0), iota((GROUP, GROUP), 1)
    causal = (rows <= cols) if backward else (cols <= rows)
    padded[...] = jnp.zeros_like(padded)

    @pl.loop(0, blocks)
    def _(k):
        at = part(k)
        padded[0:head_rows, :] = crow_ref[k]
        col = padded[...].T
        docs_row = crow_ref[k, head_rows - 1 : head_rows, :]
        allowed = (col[:, head_rows - 1 : head_rows] == docs_row) & causal
        if backward:
            scores = dot(b_ref[at, :], c_ref[at, :], NT)
        else:
            scores = dot(c_ref[at, :], b_ref[at, :], NT)
        scores = jnp.where(allowed, scores, 0.0)
        for j in range(heads // per):
            cut = slice(j * LANES, (j + 1) * LANES)
            x = x_ref[at, cut]
            base = skip_ref[:, cut] * x.astype(F32)
            top, bottom = base[:half], base[half:]
            for i in range(per):
                h = j * per + i
                own = jnp.where(lane // width == i, x, jnp.zeros_like(x))
                at_row = crow_ref[k, h : h + 1, :]
                at_col = col[:, h : h + 1]

                def weights(r, c):
                    if backward:
                        gap = at_row[:, c] - at_col[r]
                    else:
                        gap = at_col[r] - at_row[:, c]
                    return (jnp.exp2(jnp.minimum(gap, 0.0)) * scores[r, c]).astype(BF16)

                low, high, both = slice(0, half), slice(half, GROUP), slice(0, GROUP)
                if backward:
                    top = top + dot(weights(low, both), own)
                    bottom = bottom + dot(weights(high, high), own[half:])
                else:
                    top = top + dot(weights(low, low), own[:half])
                    bottom = bottom + dot(weights(high, both), own)
            low_at = pl.ds(pl.multiple_of(k * GROUP, GROUP), half)
            high_at = pl.ds(pl.multiple_of(k * GROUP + half, half), half)
            out_ref[low_at, cut] = top.astype(BF16)
            out_ref[high_at, cut] = bottom.astype(BF16)

    for copy in copies:
        copy.wait()


def inside(x, write_keys, read_keys, crow, skip, heads, backward, after, fetch=()):
    tokens, inner = x.shape
    blocks = tokens // GROUP
    return call(
        functools.partial(inside_kernel, heads, inner // heads, blocks, backward, len(fetch)),
        "inside_backward" if backward else "inside_forward",
        [pltpu.VMEM((tokens, inner), BF16)] + [pltpu.VMEM(a.shape, a.dtype) for a in fetch],
        [VM] * 6 + [HB] * len(fetch),
        (x, write_keys, read_keys, crow, skip, after, *fetch),
        scratch=[pltpu.VMEM((LANES, GROUP), F32)]
        + ([pltpu.SemaphoreType.DMA((len(fetch),))] if fetch else []),
    )


def tiling(size):
    step = next(step for step in (512, 256, LANES, size) if size % step == 0)
    return [pl.ds(j * step, step) for j in range(size // step)]


def tail_kernel(
    items, chunk, places, mixed_ref, gates_ref, read_ref, entry_ref, local_ref,
    keep_ref, other_ref, pre_ref, spread_ref, w_ref, _, *rest
):
    outs, gated = rest[:-1], rest[-1]
    at_low = places[0] == 0
    keep, other = keep_ref[...].astype(F32), other_ref[...].astype(F32)
    state = jnp.concatenate(
        [jnp.where(at_low, keep, other), jnp.where(at_low, other, keep)], axis=0
    )
    for i, item in enumerate(items):
        at = pl.ds(pl.multiple_of(places[item] * chunk, chunk), chunk)
        k = places[item] * chunk // GROUP
        entering = (local_ref[k].astype(F32) + row_at(pre_ref[...], k) * state).astype(BF16)
        carried = dot(read_ref[at, :], entering) * dot(entry_ref[at, :], spread_ref[...])
        gated[i * chunk : (i + 1) * chunk, :] = (
            (mixed_ref[at, :].astype(F32) + carried) * silu(gates_ref[at, :])
        ).astype(BF16)
    for cut in tiling(w_ref.shape[1]):
        both = dot(gated[...], w_ref[:, cut]).astype(BF16)
        for i in range(len(items)):
            outs[i][:, cut] = both[i * chunk : (i + 1) * chunk]


def forward_tail(
    chunk, items, places, mixed, gates, read_keys, entry, local, keep, other, pre, spread, out_weight, after
):
    inner, width = out_weight.shape
    count = len(items)
    return call(
        functools.partial(tail_kernel, items, chunk),
        "forward_tail",
        [pltpu.VMEM((chunk, width), BF16)] * count,
        [SM] + [VM] * 11,
        (places, mixed, gates, read_keys, entry, local, keep, other, pre, spread, out_weight, after),
        scratch=[pltpu.VMEM((count * chunk, inner), BF16)],
    )


def grad_kernel(items, chunk, first, final, places, *refs):
    count = len(items)
    go_refs, refs = refs[:count], refs[count:]
    gates_ref, read_ref, entry_ref, pre_ref, spread_ref, w_ref, _ = refs[:7]
    refs = refs[7:]
    if not first:
        sum_in, refs = refs[0], refs[3:]
    mix_ref, states_ref = refs[:2]
    summed = None if first else sum_in[...]
    for i, item in enumerate(items):
        at = pl.ds(pl.multiple_of(places[item] * chunk, chunk), chunk)
        k = places[item] * chunk // GROUP
        for cut in tiling(w_ref.shape[0]):
            grad = dot(go_refs[i][...], w_ref[cut, :], NT)
            mix_ref[at, cut] = (grad * silu(gates_ref[at, cut])).astype(BF16)
        scaled = (dot(entry_ref[at, :], spread_ref[...]) * mix_ref[at, :].astype(F32)).astype(BF16)
        state = dot(read_ref[at, :], scaled, TN)
        states_ref[places[item]] = state.astype(BF16)
        part = row_at(pre_ref[...], k) * state
        summed = part if summed is None else summed + part
    if final:
        half = summed.shape[0] // 2
        at_low = places[0] == 0
        refs[2][...] = jnp.where(at_low, summed[:half], summed[half:]).astype(BF16)
        refs[3][...] = jnp.where(at_low, summed[half:], summed[:half]).astype(BF16)
    else:
        refs[2][...] = summed


def grad_chunks(
    chunk, items, places, arrived, gates, read_keys, entry, pre, spread, out_weight, earlier, final, after
):
    count = len(arrived)
    inner = out_weight.shape[0]
    tokens = gates.shape[0]
    n = read_keys.shape[1]
    first = earlier is None
    out_shape = [pltpu.VMEM((tokens, inner), BF16), pltpu.VMEM((tokens // chunk, n, inner), BF16)]
    out_shape += [pltpu.VMEM((n // 2, inner), BF16)] * 2 if final else [pltpu.VMEM((n, inner), F32)]
    at = 1 + count + 7
    return call(
        functools.partial(grad_kernel, items, chunk, first, final),
        "grad_chunks",
        out_shape,
        [SM] + [VM] * (count + 7 + (0 if first else 3)),
        (
            places, *arrived, gates, read_keys, entry, pre, spread, out_weight, after,
            *([] if first else (earlier[2], earlier[0], earlier[1])),
        ),
        aliases=None if first else {at + 1: 0, at + 2: 1},
    )


def back_kernel(
    blocks, places, part_ref, b_ref, exit_ref, states_ref, blk_ref, keep_ref, other_ref, spread_ref,
    out_hbm, running, out_ref, out_sems,
):
    half = keep_ref.shape[0]
    per = states_ref.shape[0] // blocks
    side = places[0]
    running[pl.ds(pl.multiple_of(side * half, half), half), :] = keep_ref[...].astype(F32)
    running[pl.ds(pl.multiple_of((1 - side) * half, half), half), :] = other_ref[...].astype(F32)
    outgoing = []
    for k in reversed(range(blocks)):
        at = pl.ds(k * GROUP, GROUP)
        carried = dot(b_ref[at, :], running[...].astype(BF16)) * dot(exit_ref[at, :], spread_ref[...])
        out_ref[at, :] = (part_ref[at, :].astype(F32) + carried).astype(BF16)
        outgoing += start(out_sems.at[k], (out_ref.at[at], out_hbm.at[at]))
        if k:
            state = states_ref[k * per].astype(F32)
            for i in range(1, per):
                state = state + states_ref[k * per + i].astype(F32)
            running[...] = state + blk_ref[k : k + 1, :] * running[...]
    for copy in outgoing:
        copy.wait()


def back_tail(places, part, write_keys, exit_w, states, blk, keep, other, spread):
    tokens, inner = part.shape
    n = write_keys.shape[1]
    blocks = tokens // GROUP
    return call(
        functools.partial(back_kernel, blocks),
        "back_tail",
        [pltpu.HBM((tokens, inner), BF16)],
        [SM] + [VM] * 8,
        (places, part, write_keys, exit_w, states, blk, keep, other, spread),
        scratch=[
            pltpu.VMEM((n, inner), F32),
            pltpu.VMEM((tokens, inner), BF16),
            pltpu.SemaphoreType.DMA((blocks, 1)),
        ],
    )[0]


def shifted(block, axis, distance):
    size = lax.axis_size(axis)
    route = [(i, i + distance) for i in range(size) if 0 <= i + distance < size]
    return lax.ppermute(block, axis, route)


def swapped(block, axis):
    return lax.ppermute(block, axis, [(i, i ^ 1) for i in range(lax.axis_size(axis))])


def rotated(block, axis, distance):
    size = lax.axis_size(axis)
    return lax.ppermute(block, axis, [(i, (i + distance) % size) for i in range(size)])


def pair_kernel(places, keep_ref, got_ref, info_ref, _, tagged_ref, near_ref, facts_ref):
    low = places[0] == 0
    pick = lambda own, mate: (jnp.where(low, own, mate), jnp.where(low, mate, own))
    got, mate_raw, mate_last, mate_first = untagged(got_ref[...])
    near, far = pick(keep_ref[...].astype(F32), got)
    near_raw, far_raw = pick(info_ref[0:1, :], mate_raw)
    near_last, far_last = pick(info_ref[1:2, :], mate_last)
    near_first, far_first = pick(info_ref[2:3, :], mate_first)
    far_live = (far_first == near_last).astype(F32)
    far_decay = jnp.where(far_last == far_first, far_raw, 0.0) * far_live
    near_decay = jnp.where(near_last == near_first, near_raw, 0.0)
    half = near.shape[0]
    tagged_ref[:half, :] = (far + far_decay * near).astype(BF16)
    tagged_ref[half:, :] = tags(far_decay * near_decay, far_last, near_first)
    near_ref[...] = near.astype(BF16)
    facts_ref[...] = jnp.concatenate(
        [near_decay, far_decay, far_live, near_first, jnp.zeros((4, near.shape[1]), F32)], axis=0
    )


def enter_kernel(places, near_ref, facts_ref, one_ref, two_ref, _, *rest):
    mine_ref, hers_ref, out_ref = rest[len(rest) // 2 - 1 :][:3]
    low = places[0] == 0
    one, one_decay, one_last, one_first = untagged(one_ref[...])
    two, _, two_last, _ = untagged(two_ref[...])
    facts = facts_ref[...]
    at_near = one + jnp.where(one_first == two_last, one_decay, 0.0) * two
    near_live = (facts[3:4] == one_last).astype(F32)
    near_decay, far_decay, far_live = facts[0:1] * near_live, facts[1:2], facts[2:3]
    at_far = (near_ref[...].astype(F32) + near_decay * at_near) * far_live
    at_near = at_near * near_live
    mine_ref[...] = jnp.where(low, at_near, at_far).astype(BF16)
    hers_ref[...] = jnp.where(low, at_far, at_near).astype(BF16)
    out_ref[...] = jnp.concatenate(
        [near_decay, far_decay, near_live, far_live, jnp.zeros((4, near_decay.shape[1]), F32)], axis=0
    )


def pair_back_kernel(places, keep_ref, got_ref, facts_ref, _, tagged_ref, near_ref):
    low = places[0] == 0
    facts = facts_ref[...]
    keep, got = keep_ref[...].astype(F32), got_ref[...].astype(F32)
    near = jnp.where(low, got, keep) * facts[3:4]
    far = jnp.where(low, keep, got) * facts[2:3]
    half = near.shape[0]
    one = jnp.ones_like(facts[0:1])
    tagged_ref[:half, :] = (far + facts[0:1] * near).astype(BF16)
    tagged_ref[half:, :] = tags(facts[0:1] * facts[1:2], one, one)
    near_ref[...] = near.astype(BF16)


def enter_back_kernel(places, near_ref, facts_ref, one_ref, two_ref, _, mine_ref, hers_ref):
    low = places[0] == 0
    one, one_decay, one_last, one_first = untagged(one_ref[...])
    two, _, two_last, _ = untagged(two_ref[...])
    at_near = one + jnp.where(one_first == two_last, one_decay, 0.0) * two
    at_far = near_ref[...].astype(F32) + facts_ref[1:2, :] * at_near
    mine_ref[...] = jnp.where(low, at_far, at_near).astype(BF16)
    hers_ref[...] = jnp.where(low, at_near, at_far).astype(BF16)


def small(kernel, name, shapes, args, after, through=()):
    out_shape = [pltpu.VMEM(dims, kind) for dims, kind in shapes]
    out_shape += [pltpu.VMEM(a.shape, a.dtype) for a in through]
    count = len(args) + 1
    return call(
        kernel, name, out_shape, [SM] + [VM] * (len(args) + len(through)), (*args, after, *through),
        aliases={count + i: len(shapes) + i for i in range(len(through))},
    )


def between_pairs(tagged, way):
    half = tagged.shape[0] - TILE
    window = max(lax.axis_size("seq") // 4, 1)
    if window <= 2:
        one = shifted(tagged, "seq", 2 * way)
        return one, shifted(tagged, "seq", 4 * way) if window == 2 else jnp.zeros_like(one)
    total, decay, _, first = untagged(tagged)
    came, _, came_last, _ = untagged(shifted(tagged, "seq", 2 * way))
    decay = jnp.where(first == came_last, decay, 0.0)
    total = (total + decay * came).astype(BF16)
    reach = 2
    while reach < window:
        decay = decay * shifted(decay, "seq", way * reach)
        total = (total.astype(F32) + decay * shifted(total, "seq", 2 * way * reach).astype(F32)).astype(BF16)
        reach *= 2
    one = shifted(jnp.concatenate([total, tagged[half:]], axis=0), "seq", 2 * way)
    return one, jnp.zeros_like(one)


def shards(
    inputs, gates, write_keys, read_keys, log_decay, skip_gain, doc_ids, out_weight, grad_out
):
    tokens, inner = inputs.shape
    heads = log_decay.shape[0]
    width = inner // heads
    members = lax.axis_size("head")
    chips = members // 2
    chunk = tokens // members
    here = lax.axis_index("head")
    chip, core = here // 2, here % 2
    mate = here ^ 1
    side = lax.axis_index("seq") % 2
    numbers = [here, mate]
    for d in range(1, chips):
        source = (here - 2 * d) % members
        target = ((chip + d) % chips) * 2
        numbers += [source, source ^ 1, target + 1 - core, target + core]
    places = jnp.stack([side] + numbers).astype(jnp.int32)

    remote = [rotated(grad_out, "head", 2 * d) for d in range(1, chips)]
    sibling = swapped(grad_out, "head")

    spread = (
        jnp.arange(LANES)[:, None] == (jnp.arange(inner) // width)[None, :]
    ).astype(BF16)
    skip = jnp.repeat(skip_gain, width)[None, :]
    crow, entry, exit_w, local, keep, send, pre, blk, info, x, b, c = local_states(
        places, inputs, write_keys, read_keys, log_decay, doc_ids[None, :], spread
    )
    half, tagged, facts_shape = keep.shape, send.shape, info.shape
    mixed, gates, weight, own_grad = inside(
        x, b, c, crow, skip, heads, False, send, (gates, out_weight, grad_out)
    )
    pair, near, facts = small(
        pair_kernel, "pair", [(tagged, BF16), (half, BF16), (facts_shape, F32)],
        (places, keep, swapped(send, "seq"), info), mixed,
    )
    one, two = between_pairs(pair, 1)

    def grads(items, arrived, earlier, final, after):
        return grad_chunks(
            chunk, items, places, arrived, gates, c, entry, pre, spread, weight, earlier, final, after
        )

    back = grads((1, 2), [own_grad, sibling], None, chips == 1, pair)
    enter_keep, hers, facts, *remote = small(
        enter_kernel, "enter", [(half, BF16), (half, BF16), (facts_shape, F32)],
        (places, near, facts, one, two), back[1], remote,
    )
    enter_other = swapped(hers, "seq")

    def tail(items, after):
        return forward_tail(
            chunk, items, places, mixed, gates, c, entry, local, enter_keep, enter_other, pre, spread,
            weight, after,
        )

    after = hers
    for d in range(chips - 1):
        relayed = swapped(remote[d], "head")
        back = grads((3 + 4 * d,), [remote[d]], back, False, after)
        back = grads((4 + 4 * d,), [relayed], back, d == chips - 2, back[1])
        after = back[1]
    mix, states, back_keep, back_send = back
    got = swapped(back_send, "seq")
    landed = []
    after = back_send
    for d in range(chips - 1):
        give, stay = tail((5 + 4 * d, 6 + 4 * d), after)
        both = (stay.astype(F32) + swapped(give, "head").astype(F32)).astype(BF16)
        landed.append(rotated(both, "head", 2 * (d + 1)))
        after = give
    pair, near = small(
        pair_back_kernel, "pair_back", [(tagged, BF16), (half, BF16)],
        (places, back_keep, got, facts), after,
    )
    one, two = between_pairs(pair, -1)
    give, stay = tail((2, 1), pair)
    arrive_keep, hers = small(
        enter_back_kernel, "enter_back", [(half, BF16), (half, BF16)],
        (places, near, facts, one, two), give,
    )
    arrive_other = swapped(hers, "seq")
    part = inside(mix, b, c, crow, skip, heads, True, hers)[0]
    out = stay.astype(F32) + swapped(give, "head").astype(F32)
    for block in landed:
        out = out + block.astype(F32)
    grad_inputs = back_tail(
        places, part, b, exit_w, states, blk, arrive_keep, arrive_other, spread
    )
    return out.astype(BF16), grad_inputs


def solution(mesh):
    in_specs = (
        P("seq", "head"),
        P("seq", "head"),
        P("seq", None),
        P("seq", None),
        P("head", "seq"),
        P("head"),
        P("seq"),
        P("head", None),
        P(("seq", "head"), None),
    )
    out_specs = (P(("seq", "head"), None), P("seq", "head"))
    return jax.shard_map(shards, mesh=mesh, in_specs=in_specs, out_specs=out_specs, check_vma=False)
```

```python
import functools
import math

import jax
import jax.numpy as jnp
from jax import lax
from jax.experimental import pallas as pl
from jax.experimental.pallas import tpu as pltpu
from jax.sharding import PartitionSpec as P

GROUP = 256
LANES = 128
TILE = 16
LOG2E = math.log2(math.e)
F32 = jnp.float32
BF16 = jnp.bfloat16
NT = (((1,), (1,)), ((), ()))
TN = (((0,), (0,)), ((), ()))
VM = pl.BlockSpec(memory_space=pltpu.VMEM)
SM = pl.BlockSpec(memory_space=pltpu.SMEM)
HB = pl.BlockSpec(memory_space=pltpu.HBM)
DECAY, DECAY_REST, LAST, FIRST = range(4)


def dot(a, b, dims=(((1,), (0,)), ((), ()))):
    return lax.dot_general(a, b, dims, preferred_element_type=F32)


def call(kernel, name, out_shape, in_specs, args, limit_mib=12, scratch=(), aliases=None, flops=1):
    space = {id(VM): pltpu.VMEM, id(HB): pltpu.HBM}
    args = [
        arg if spec is SM else pltpu.with_memory_space_constraint(arg, space[id(spec)])
        for spec, arg in zip(in_specs, args, strict=True)
    ]
    return pl.pallas_call(
        kernel,
        in_specs=in_specs,
        out_specs=[VM if o.memory_space == pltpu.VMEM else HB for o in out_shape],
        out_shape=out_shape,
        scratch_shapes=scratch,
        input_output_aliases=aliases or {},
        compiler_params=pltpu.CompilerParams(vmem_limit_bytes=limit_mib * 2**20),
        cost_estimate=pl.CostEstimate(flops=int(flops), bytes_accessed=1, transcendentals=0),
        name=name,
    )(*args)


def start(sems, *pairs):
    copies = [
        pltpu.make_async_copy(source, target, sems.at[i]) for i, (source, target) in enumerate(pairs)
    ]
    for copy in copies:
        copy.start()
    return copies


def split(value):
    high = value.astype(BF16)
    return high, (value - high.astype(F32)).astype(BF16)


def silu(gates):
    v = gates.astype(F32)
    return 0.5 * v * (1.0 + jnp.tanh(0.5 * v))


def row_at(rows, k):
    return jnp.sum(jnp.where(iota(rows.shape, 0) == k, rows, 0.0), axis=0, keepdims=True)


def iota(shape, dim):
    return lax.broadcasted_iota(jnp.int32, shape, dim)


def state_kernel(
    heads, blocks, places, x_hbm, b_hbm, c_hbm, ld_hbm, doc_ref, spread_ref,
    crow_ref, entry_ref, exit_ref, local_ref, keep_ref, send_ref, pre_ref, blk_ref, info_ref,
    b_ref, c_ref, padded, running, ld_ref, x_ref, sems,
):
    n, inner = running.shape
    half = n // 2
    parts = [pl.ds(k * GROUP, GROUP) for k in range(blocks)]
    ld_copy, b_copy, c_copy, *x_copies = start(
        sems, (ld_hbm, ld_ref), (b_hbm, b_ref), (c_hbm, c_ref),
        *[(x_hbm.at[p], x_ref.at[p]) for p in parts],
    )
    head_rows = crow_ref.shape[1]
    spread = spread_ref[...]
    later = (iota((GROUP, GROUP), 0) <= iota((GROUP, GROUP), 1)).astype(BF16)
    padded[...] = jnp.zeros_like(padded)
    row = iota((head_rows, GROUP), 0)
    pre_ref[...] = jnp.zeros_like(pre_ref)
    blk_ref[...] = jnp.zeros_like(blk_ref)
    info_ref[...] = jnp.zeros_like(info_ref)
    first_doc = last_doc = total = None
    ld_copy.wait()
    for k in range(blocks):
        at = slice(k * GROUP, (k + 1) * GROUP)
        padded[0:heads, :] = ld_ref[:, at] * LOG2E
        steps = padded[0:head_rows, :]
        high, rest = split(steps)
        mid, low = split(steps - high.astype(F32))
        cum = dot(high, later) + (dot(mid, later) + dot(low, later))
        cum = jnp.where(row == head_rows - 1, doc_ref[:, at].astype(F32), cum)
        crow_ref[k] = cum
        padded[0:head_rows, :] = cum
        ccol = padded[...].T
        padded[0:head_rows, :] = jnp.zeros((head_rows, GROUP), F32)
        docs = ccol[:, head_rows - 1 : head_rows]
        end = ccol[GROUP - 1 :]
        end_doc = end[:, head_rows - 1 : head_rows]
        if k == 0:
            first_doc = ccol[0:1, head_rows - 1 : head_rows]
            last_doc = first_doc
            total = jnp.zeros_like(end)
        exit_w = jnp.where(docs == end_doc, jnp.exp2(jnp.minimum(end - ccol, 0.0)), 0.0).astype(BF16)
        exit_ref[at, :] = exit_w
        entry_ref[at, :] = jnp.where(docs == last_doc, jnp.exp2(jnp.minimum(ccol, 0.0)), 0.0).astype(BF16)
        if k == 0:
            b_copy.wait()
        x_copies[k].wait()
        scaled = (dot(exit_w, spread) * x_ref[at, :].astype(F32)).astype(BF16)
        own = dot(b_ref[at, :], scaled, TN)
        block_decay = jnp.where(end_doc == last_doc, jnp.exp2(end), 0.0)
        whole = jnp.exp2(total + end)
        stacked = jnp.concatenate(
            [block_decay, jnp.where(end_doc == first_doc, whole, 0.0), whole, jnp.zeros((5, LANES), F32)],
            axis=0,
        )
        high, rest = split(stacked)
        wide = dot(high, spread) + dot(rest, spread)
        blk_ref[k : k + 1, :] = wide[0:1]
        if k == 0:
            local_ref[k] = jnp.zeros((n, inner), BF16)
            pre_ref[0:1, :] = jnp.ones((1, inner), F32)
            running[...] = own
        else:
            local_ref[k] = running[...].astype(BF16)
            running[...] = wide[0:1] * running[...] + own
        if k < blocks - 1:
            pre_ref[k + 1 : k + 2, :] = wide[1:2]
        total = total + end
        last_doc = end_doc
    raw = wide[2:3]
    last_row = jnp.broadcast_to(last_doc + 1.0, (1, inner))
    first_row = jnp.broadcast_to(first_doc + 1.0, (1, inner))
    info_ref[0:1, :] = raw
    info_ref[1:2, :] = last_row
    info_ref[2:3, :] = first_row
    side = places[0]
    keep_ref[...] = running[pl.ds(pl.multiple_of(side * half, half), half), :].astype(BF16)
    send_ref[0:half, :] = running[pl.ds(pl.multiple_of((1 - side) * half, half), half), :].astype(BF16)
    send_ref[half:, :] = tags(raw, last_row, first_row)
    c_copy.wait()


def tags(decay, last, first):
    high, rest = split(decay)
    rows = [high.astype(F32), rest.astype(F32), last, first]
    rows.append(jnp.zeros((TILE - len(rows), decay.shape[1]), F32))
    return jnp.concatenate(rows, axis=0).astype(BF16)


def untagged(block):
    half = block.shape[0] - TILE
    state, rows = block[:half].astype(F32), block[half:].astype(F32)
    row = lambda i: rows[i : i + 1]
    return state, row(DECAY) + row(DECAY_REST), row(LAST), row(FIRST)


def local_states(places, inputs, write_keys, read_keys, log_decay, docs_row, spread):
    tokens, inner = inputs.shape
    heads = log_decay.shape[0]
    n = write_keys.shape[1]
    blocks = tokens // GROUP
    head_rows = -(-(heads + 1) // 8) * 8
    block_rows = -(-blocks // 8) * 8
    return call(
        functools.partial(state_kernel, heads, blocks),
        "local_states",
        [
            pltpu.VMEM((blocks, head_rows, GROUP), F32),
            pltpu.VMEM((tokens, LANES), BF16),
            pltpu.VMEM((tokens, LANES), BF16),
            pltpu.VMEM((blocks, n, inner), BF16),
            pltpu.VMEM((n // 2, inner), BF16),
            pltpu.VMEM((n // 2 + TILE, inner), BF16),
            pltpu.VMEM((block_rows, inner), F32),
            pltpu.VMEM((block_rows, inner), F32),
            pltpu.VMEM((8, inner), F32),
            pltpu.VMEM((tokens, n), BF16),
            pltpu.VMEM((tokens, n), BF16),
        ],
        [SM] + [HB] * 4 + [VM] * 2,
        (places, inputs, write_keys, read_keys, log_decay, docs_row, spread),
        scratch=[
            pltpu.VMEM((LANES, GROUP), F32),
            pltpu.VMEM((n, inner), F32),
            pltpu.VMEM((heads, tokens), F32),
            pltpu.VMEM((tokens, inner), BF16),
            pltpu.SemaphoreType.DMA((3 + blocks,)),
        ],
    )


def inside_kernel(
    heads, width, blocks, backward, fetched, chips, which, places,
    x_ref, b_ref, c_ref, crow_ref, skip_ref, _, *rest
):
    per_chip = blocks // chips
    if backward and which[0]:
        rest = rest[1:]
    fetch_hbm, out_ref, fetch_vm, padded = (
        rest[:fetched], rest[fetched], rest[fetched + 1 : 2 * fetched + 1], rest[2 * fetched + 1]
    )
    half = GROUP // 2
    head_rows = crow_ref.shape[1]
    per = LANES // width
    part = lambda k: pl.ds(pl.multiple_of(k * GROUP, GROUP), GROUP)
    copies = []
    if not backward:
        sems, x_sems, x_hbm, x_ref = *rest[2 * fetched + 2 : 2 * fetched + 4], x_ref, rest[-1]
        incoming = lambda k: pltpu.make_async_copy(x_hbm.at[part(k)], x_ref.at[part(k)], x_sems.at[k])
        for k in range(blocks):
            incoming(k).start()
        copies = start(sems, *zip(fetch_hbm, fetch_vm))
    lane = iota((GROUP, LANES), 1)
    rows, cols = iota((GROUP, GROUP), 0), iota((GROUP, GROUP), 1)
    causal = (rows <= cols) if backward else (cols <= rows)
    padded[...] = jnp.zeros_like(padded)

    @pl.loop(which[0] * per_chip, which[1] * per_chip)
    def _(step):
        k = step
        if backward:
            turn = places[1] // 2 + step // per_chip
            k = lax.rem(turn, chips) * per_chip + lax.rem(step, per_chip)
        at = part(k)
        padded[0:head_rows, :] = crow_ref[k]
        col = padded[...].T
        docs_row = crow_ref[k, head_rows - 1 : head_rows, :]
        allowed = (col[:, head_rows - 1 : head_rows] == docs_row) & causal
        if backward:
            scores = dot(b_ref[at, :], c_ref[at, :], NT)
        else:
            scores = dot(c_ref[at, :], b_ref[at, :], NT)
        scores = jnp.where(allowed, scores, 0.0)
        if not backward:
            incoming(k).wait()
        for j in range(heads // per):
            cut = slice(j * LANES, (j + 1) * LANES)
            x = x_ref[at, cut]
            base = skip_ref[:, cut] * x.astype(F32)
            top, bottom = base[:half], base[half:]
            for i in range(per):
                h = j * per + i
                own = jnp.where(lane // width == i, x, jnp.zeros_like(x))
                at_row = crow_ref[k, h : h + 1, :]
                at_col = col[:, h : h + 1]

                def weights(r, c):
                    if backward:
                        gap = at_row[:, c] - at_col[r]
                    else:
                        gap = at_col[r] - at_row[:, c]
                    return (jnp.exp2(jnp.minimum(gap, 0.0)) * scores[r, c]).astype(BF16)

                low, high, both = slice(0, half), slice(half, GROUP), slice(0, GROUP)
                if backward:
                    top = top + dot(weights(low, both), own)
                    bottom = bottom + dot(weights(high, high), own[half:])
                else:
                    top = top + dot(weights(low, low), own[:half])
                    bottom = bottom + dot(weights(high, both), own)
            low_at = pl.ds(pl.multiple_of(k * GROUP, GROUP), half)
            high_at = pl.ds(pl.multiple_of(k * GROUP + half, half), half)
            out_ref[low_at, cut] = top.astype(BF16)
            out_ref[high_at, cut] = bottom.astype(BF16)

    for copy in copies:
        copy.wait()


def inside(places, x, write_keys, read_keys, crow, skip, heads, after, fetch=(), which=None, earlier=None):
    tokens, inner = x.shape
    blocks = tokens // GROUP
    backward = which is not None
    chips = lax.axis_size("head") // 2 if backward else 1
    carried = [] if earlier is None else [earlier]
    return call(
        functools.partial(
            inside_kernel, heads, inner // heads, blocks, backward, len(fetch), chips, which or (0, 1)
        ),
        "inside_backward" if backward else "inside_forward",
        [pltpu.VMEM((tokens, inner), BF16)] + [pltpu.VMEM(a.shape, a.dtype) for a in fetch],
        [SM] + [VM if backward else HB] + [VM] * (5 + len(carried)) + [HB] * len(fetch),
        (places, x, write_keys, read_keys, crow, skip, after, *carried, *fetch),
        scratch=[pltpu.VMEM((LANES, GROUP), F32)]
        + ([] if backward else [
            pltpu.SemaphoreType.DMA((len(fetch),)),
            pltpu.SemaphoreType.DMA((blocks,)),
            pltpu.VMEM((tokens, inner), BF16),
        ]),
        aliases={7: 0} if carried else None,
    )


def tiling(size):
    step = next(step for step in (512, 256, LANES, size) if size % step == 0)
    return [pl.ds(j * step, step) for j in range(size // step)]


def tail_kernel(
    items, chunk, places, mixed_ref, gates_ref, read_ref, entry_ref, local_ref,
    keep_ref, other_ref, pre_ref, spread_ref, w_ref, *rest
):
    cuts = tiling(w_ref.shape[1])
    outs, gated = rest[len(rest) - 2 - len(cuts) : -1], rest[-1]
    at_low = places[0] == 0
    keep, other = keep_ref[...].astype(F32), other_ref[...].astype(F32)
    state = jnp.concatenate(
        [jnp.where(at_low, keep, other), jnp.where(at_low, other, keep)], axis=0
    )
    for i, item in enumerate(items):
        at = pl.ds(pl.multiple_of(places[item] * chunk, chunk), chunk)
        k = places[item] * chunk // GROUP
        entering = (local_ref[k].astype(F32) + row_at(pre_ref[...], k) * state).astype(BF16)
        carried = dot(read_ref[at, :], entering) * dot(entry_ref[at, :], spread_ref[...])
        gated[i * chunk : (i + 1) * chunk, :] = (
            (mixed_ref[at, :].astype(F32) + carried) * silu(gates_ref[at, :])
        ).astype(BF16)
    for j, cut in enumerate(cuts):
        both = dot(gated[...], w_ref[:, cut]).astype(BF16)
        outs[j][...] = both[:chunk]
        outs[-1][:, cut] = both[chunk:]


def forward_tail(
    chunk, items, places, mixed, gates, read_keys, entry, local, keep, other, pre, spread, out_weight, after
):
    inner, width = out_weight.shape
    count = len(items)
    return call(
        functools.partial(tail_kernel, items, chunk),
        "forward_tail",
        [pltpu.VMEM((chunk, cut.size), BF16) for cut in tiling(width)] + [pltpu.VMEM((chunk, width), BF16)],
        [SM] + [VM] * (10 + len(after)),
        (places, mixed, gates, read_keys, entry, local, keep, other, pre, spread, out_weight, *after),
        scratch=[pltpu.VMEM((count * chunk, inner), BF16)],
    )


def sum_kernel(count, final, *refs):
    stay_ref, piece_refs, landed_refs = refs[0], refs[1 : 1 + count], refs[1 + count : len(refs) - 1 - 2 * final]
    out_ref = refs[-2] if final else refs[-1]
    outgoing = []
    for j, cut in enumerate(tiling(stay_ref.shape[1])):
        total = stay_ref[:, cut].astype(F32) + piece_refs[j][...].astype(F32)
        for ref in landed_refs:
            total = total + ref[:, cut].astype(F32)
        out_ref[:, cut] = total.astype(BF16)
        if final:
            outgoing += start(refs[-1].at[j], (out_ref.at[:, cut], refs[-3].at[:, cut]))
    for copy in outgoing:
        copy.wait()


def chunk_sum(stay, pieces, landed=(), final=False):
    make = pltpu.HBM if final else pltpu.VMEM
    return call(
        functools.partial(sum_kernel, len(pieces), final),
        "chunk_sum",
        [make(stay.shape, stay.dtype)],
        [VM] * (1 + len(pieces) + len(landed)),
        (stay, *pieces, *landed),
        scratch=[
            pltpu.VMEM(stay.shape, stay.dtype), pltpu.SemaphoreType.DMA((len(pieces), 1))
        ] if final else (),
    )[0]


def grad_kernel(items, chunk, first, final, places, *refs):
    count = len(items)
    go_refs, refs = refs[:count], refs[count:]
    gates_ref, read_ref, entry_ref, pre_ref, spread_ref, w_ref, _ = refs[:7]
    refs = refs[7:]
    if not first:
        sum_in, refs = refs[0], refs[3:]
    mix_ref, states_ref = refs[:2]
    summed = None if first else sum_in[...]
    for i, item in enumerate(items):
        at = pl.ds(pl.multiple_of(places[item] * chunk, chunk), chunk)
        k = places[item] * chunk // GROUP
        for cut in tiling(w_ref.shape[0]):
            grad = dot(go_refs[i][...], w_ref[cut, :], NT)
            mix_ref[at, cut] = (grad * silu(gates_ref[at, cut])).astype(BF16)
        scaled = (dot(entry_ref[at, :], spread_ref[...]) * mix_ref[at, :].astype(F32)).astype(BF16)
        state = dot(read_ref[at, :], scaled, TN)
        states_ref[places[item]] = state.astype(BF16)
        part = row_at(pre_ref[...], k) * state
        summed = part if summed is None else summed + part
    if final:
        half = summed.shape[0] // 2
        at_low = places[0] == 0
        refs[2][...] = jnp.where(at_low, summed[:half], summed[half:]).astype(BF16)
        refs[3][...] = jnp.where(at_low, summed[half:], summed[:half]).astype(BF16)
    else:
        refs[2][...] = summed


def grad_chunks(
    chunk, items, places, arrived, gates, read_keys, entry, pre, spread, out_weight, earlier, final, after
):
    count = len(arrived)
    inner = out_weight.shape[0]
    tokens = gates.shape[0]
    n = read_keys.shape[1]
    first = earlier is None
    out_shape = [pltpu.VMEM((tokens, inner), BF16), pltpu.VMEM((tokens // chunk, n, inner), BF16)]
    out_shape += [pltpu.VMEM((n // 2, inner), BF16)] * 2 if final else [pltpu.VMEM((n, inner), F32)]
    at = 1 + count + 7
    return call(
        functools.partial(grad_kernel, items, chunk, first, final),
        "grad_chunks",
        out_shape,
        [SM] + [VM] * (count + 7 + (0 if first else 3)),
        (
            places, *arrived, gates, read_keys, entry, pre, spread, out_weight, after,
            *([] if first else (earlier[2], earlier[0], earlier[1])),
        ),
        aliases=None if first else {at + 1: 0, at + 2: 1},
    )


def back_kernel(
    blocks, places, part_ref, b_ref, exit_ref, states_ref, blk_ref, keep_ref, other_ref, spread_ref,
    out_hbm, running, out_ref, out_sems,
):
    half = keep_ref.shape[0]
    per = states_ref.shape[0] // blocks
    side = places[0]
    running[pl.ds(pl.multiple_of(side * half, half), half), :] = keep_ref[...].astype(F32)
    running[pl.ds(pl.multiple_of((1 - side) * half, half), half), :] = other_ref[...].astype(F32)
    outgoing = []
    for k in reversed(range(blocks)):
        at = pl.ds(k * GROUP, GROUP)
        carried = dot(b_ref[at, :], running[...].astype(BF16)) * dot(exit_ref[at, :], spread_ref[...])
        out_ref[at, :] = (part_ref[at, :].astype(F32) + carried).astype(BF16)
        outgoing += start(out_sems.at[k], (out_ref.at[at], out_hbm.at[at]))
        if k:
            state = states_ref[k * per].astype(F32)
            for i in range(1, per):
                state = state + states_ref[k * per + i].astype(F32)
            running[...] = state + blk_ref[k : k + 1, :] * running[...]
    for copy in outgoing:
        copy.wait()


def back_tail(places, part, write_keys, exit_w, states, blk, keep, other, spread):
    tokens, inner = part.shape
    n = write_keys.shape[1]
    blocks = tokens // GROUP
    return call(
        functools.partial(back_kernel, blocks),
        "back_tail",
        [pltpu.HBM((tokens, inner), BF16)],
        [SM] + [VM] * 8,
        (places, part, write_keys, exit_w, states, blk, keep, other, spread),
        scratch=[
            pltpu.VMEM((n, inner), F32),
            pltpu.VMEM((tokens, inner), BF16),
            pltpu.SemaphoreType.DMA((blocks, 1)),
        ],
    )[0]


def shifted(block, axis, distance):
    size = lax.axis_size(axis)
    route = [(i, i + distance) for i in range(size) if 0 <= i + distance < size]
    return lax.ppermute(block, axis, route)


def swapped(block, axis):
    return lax.ppermute(block, axis, [(i, i ^ 1) for i in range(lax.axis_size(axis))])


def rotated(block, axis, distance):
    size = lax.axis_size(axis)
    return lax.ppermute(block, axis, [(i, (i + distance) % size) for i in range(size)])


def pair_kernel(places, keep_ref, got_ref, info_ref, _, tagged_ref, near_ref, facts_ref):
    low = places[0] == 0
    pick = lambda own, mate: (jnp.where(low, own, mate), jnp.where(low, mate, own))
    got, mate_raw, mate_last, mate_first = untagged(got_ref[...])
    near, far = pick(keep_ref[...].astype(F32), got)
    near_raw, far_raw = pick(info_ref[0:1, :], mate_raw)
    near_last, far_last = pick(info_ref[1:2, :], mate_last)
    near_first, far_first = pick(info_ref[2:3, :], mate_first)
    far_live = (far_first == near_last).astype(F32)
    far_decay = jnp.where(far_last == far_first, far_raw, 0.0) * far_live
    near_decay = jnp.where(near_last == near_first, near_raw, 0.0)
    half = near.shape[0]
    tagged_ref[:half, :] = (far + far_decay * near).astype(BF16)
    tagged_ref[half:, :] = tags(far_decay * near_decay, far_last, near_first)
    near_ref[...] = near.astype(BF16)
    facts_ref[...] = jnp.concatenate(
        [near_decay, far_decay, far_live, near_first, jnp.zeros((4, near.shape[1]), F32)], axis=0
    )


def enter_kernel(through, places, near_ref, facts_ref, one_ref, two_ref, _, *rest):
    copies = start(rest[-1], *zip(rest[:through], rest[through + 3 :])) if through else []
    mine_ref, hers_ref, out_ref = rest[through : through + 3]
    low = places[0] == 0
    one, one_decay, one_last, one_first = untagged(one_ref[...])
    two, _, two_last, _ = untagged(two_ref[...])
    facts = facts_ref[...]
    at_near = one + jnp.where(one_first == two_last, one_decay, 0.0) * two
    near_live = (facts[3:4] == one_last).astype(F32)
    near_decay, far_decay, far_live = facts[0:1] * near_live, facts[1:2], facts[2:3]
    at_far = (near_ref[...].astype(F32) + near_decay * at_near) * far_live
    at_near = at_near * near_live
    mine_ref[...] = jnp.where(low, at_near, at_far).astype(BF16)
    hers_ref[...] = jnp.where(low, at_far, at_near).astype(BF16)
    out_ref[...] = jnp.concatenate(
        [near_decay, far_decay, near_live, far_live, jnp.zeros((4, near_decay.shape[1]), F32)], axis=0
    )
    for copy in copies:
        copy.wait()


def pair_back_kernel(places, keep_ref, got_ref, facts_ref, _, *rest):
    tagged_ref, near_ref = rest[len(rest) // 2 - 1 :][:2]
    low = places[0] == 0
    facts = facts_ref[...]
    keep, got = keep_ref[...].astype(F32), got_ref[...].astype(F32)
    near = jnp.where(low, got, keep) * facts[3:4]
    far = jnp.where(low, keep, got) * facts[2:3]
    half = near.shape[0]
    one = jnp.ones_like(facts[0:1])
    tagged_ref[:half, :] = (far + facts[0:1] * near).astype(BF16)
    tagged_ref[half:, :] = tags(facts[0:1] * facts[1:2], one, one)
    near_ref[...] = near.astype(BF16)


def enter_back_kernel(places, near_ref, facts_ref, one_ref, two_ref, _, *rest):
    mine_ref, hers_ref = rest[len(rest) // 2 - 1 :][:2]
    low = places[0] == 0
    one, one_decay, one_last, one_first = untagged(one_ref[...])
    two, _, two_last, _ = untagged(two_ref[...])
    at_near = one + jnp.where(one_first == two_last, one_decay, 0.0) * two
    at_far = near_ref[...].astype(F32) + facts_ref[1:2, :] * at_near
    mine_ref[...] = jnp.where(low, at_far, at_near).astype(BF16)
    hers_ref[...] = jnp.where(low, at_near, at_far).astype(BF16)


def small(kernel, name, shapes, args, after, through=(), kept=()):
    out_shape = [pltpu.VMEM(dims, kind) for dims, kind in shapes]
    out_shape += [pltpu.VMEM(a.shape, a.dtype) for a in (*through, *kept)]
    count = 1 + len(args) + len(through)
    return call(
        kernel, name, out_shape, [SM] + [VM] * len(args) + [HB] * len(through) + [VM] * len(kept),
        (*args, after, *through, *kept),
        aliases={count + i: len(shapes) + i for i in range(len(kept))},
        scratch=[pltpu.SemaphoreType.DMA((len(through),))] if through else (),
    )


def between_pairs(tagged, way):
    half = tagged.shape[0] - TILE
    window = max(lax.axis_size("seq") // 4, 1)
    if window <= 2:
        one = shifted(tagged, "seq", 2 * way)
        return one, shifted(tagged, "seq", 4 * way) if window == 2 else jnp.zeros_like(one)
    total, decay, _, first = untagged(tagged)
    came, _, came_last, _ = untagged(shifted(tagged, "seq", 2 * way))
    decay = jnp.where(first == came_last, decay, 0.0)
    total = (total + decay * came).astype(BF16)
    reach = 2
    while reach < window:
        decay = decay * shifted(decay, "seq", way * reach)
        total = (total.astype(F32) + decay * shifted(total, "seq", 2 * way * reach).astype(F32)).astype(BF16)
        reach *= 2
    one = shifted(jnp.concatenate([total, tagged[half:]], axis=0), "seq", 2 * way)
    return one, jnp.zeros_like(one)


def shards(
    inputs, gates, write_keys, read_keys, log_decay, skip_gain, doc_ids, out_weight, grad_out
):
    tokens, inner = inputs.shape
    heads = log_decay.shape[0]
    width = inner // heads
    members = lax.axis_size("head")
    chips = members // 2
    chunk = tokens // members
    here = lax.axis_index("head")
    chip, core = here // 2, here % 2
    mate = here ^ 1
    side = lax.axis_index("seq") % 2
    numbers = [here, mate]
    for d in range(1, chips):
        source = (here - 2 * d) % members
        target = ((chip + d) % chips) * 2
        numbers += [source, source ^ 1, target + 1 - core, target + core]
    places = jnp.stack([side] + numbers).astype(jnp.int32)

    remote = [rotated(grad_out, "head", 2 * d) for d in range(1, chips)]
    sibling = swapped(grad_out, "head")

    spread = (
        jnp.arange(LANES)[:, None] == (jnp.arange(inner) // width)[None, :]
    ).astype(BF16)
    skip = jnp.repeat(skip_gain, width)[None, :]
    crow, entry, exit_w, local, keep, send, pre, blk, info, b, c = local_states(
        places, inputs, write_keys, read_keys, log_decay, doc_ids[None, :], spread
    )
    half, tagged, facts_shape = keep.shape, send.shape, info.shape
    mixed, gates, weight, own_grad = inside(
        places, inputs, b, c, crow, skip, heads, send, (gates, out_weight, grad_out)
    )
    pair, near, facts = small(
        pair_kernel, "pair", [(tagged, BF16), (half, BF16), (facts_shape, F32)],
        (places, keep, swapped(send, "seq"), info), mixed,
    )
    one, two = between_pairs(pair, 1)

    def grads(items, arrived, earlier, final, after):
        return grad_chunks(
            chunk, items, places, arrived, gates, c, entry, pre, spread, weight, earlier, final, after
        )

    back = grads((1, 2), [own_grad, sibling], None, chips == 1, pair)
    part = inside(places, back[0], b, c, crow, skip, heads, back[1], which=(0, 1))[0]
    enter_keep, hers, facts, *remote = small(
        functools.partial(enter_kernel, len(remote)), "enter", [(half, BF16), (half, BF16), (facts_shape, F32)],
        (places, near, facts, one, two), part, remote,
    )
    enter_other = swapped(hers, "seq")

    def tail(items, *after):
        return forward_tail(
            chunk, items, places, mixed, gates, c, entry, local, enter_keep, enter_other, pre, spread,
            weight, after,
        )

    for d in range(chips - 1):
        relayed = swapped(remote[d], "head")
        back = grads((3 + 4 * d,), [remote[d]], back, False, hers)
        back = grads((4 + 4 * d,), [relayed], back, d == chips - 2, back[1])
    mix, states, back_keep, back_send = back
    got = swapped(back_send, "seq")
    after, given, stayed = back_send, [], []
    for d in range(chips - 1):
        *give, after = tail((5 + 4 * d, 6 + 4 * d), after)
        given += give
        stayed.append(after)
    pair, near, *given = small(
        pair_back_kernel, "pair_back", [(tagged, BF16), (half, BF16)],
        (places, back_keep, got, facts), after, kept=given,
    )
    one, two = between_pairs(pair, -1)
    landed, pieces = [], len(given) // max(chips - 1, 1)
    for d in range(chips - 1):
        got = [swapped(piece, "head") for piece in given[d * pieces : (d + 1) * pieces]]
        after = chunk_sum(stayed[d], got)
        landed.append(rotated(after, "head", 2 * (d + 1)))
    *give, stay = tail((2, 1), pair, after)
    part = inside(places, mix, b, c, crow, skip, heads, stay, which=(1, chips), earlier=part)[0]
    arrive_keep, hers, *give = small(
        enter_back_kernel, "enter_back", [(half, BF16), (half, BF16)],
        (places, near, facts, one, two), part, kept=give,
    )
    arrive_other = swapped(hers, "seq")
    out = chunk_sum(stay, [swapped(piece, "head") for piece in give], landed, True)
    grad_inputs = back_tail(
        places, part, b, exit_w, states, blk, arrive_keep, arrive_other, spread
    )
    return out, grad_inputs


def solution(mesh):
    in_specs = (
        P("seq", "head"),
        P("seq", "head"),
        P("seq", None),
        P("seq", None),
        P("head", "seq"),
        P("head"),
        P("seq"),
        P("head", None),
        P(("seq", "head"), None),
    )
    out_specs = (P(("seq", "head"), None), P("seq", "head"))
    return jax.shard_map(shards, mesh=mesh, in_specs=in_specs, out_specs=out_specs, check_vma=False)
```

```python
import functools
import math

import jax
import jax.numpy as jnp
from jax import lax
from jax.experimental import pallas as pl
from jax.experimental.pallas import tpu as pltpu
from jax.sharding import PartitionSpec as P

GROUP = 256
LANES = 128
TILE = 16
PARTS = 4
HALVES = 1
TAIL_COST, FAR_COST, NEAR_COST = 1.73e9, 2.306e10, 9.224e9
LOG2E = math.log2(math.e)
F32 = jnp.float32
BF16 = jnp.bfloat16
NT = (((1,), (1,)), ((), ()))
TN = (((0,), (0,)), ((), ()))
VM = pl.BlockSpec(memory_space=pltpu.VMEM)
SM = pl.BlockSpec(memory_space=pltpu.SMEM)
HB = pl.BlockSpec(memory_space=pltpu.HBM)
DECAY, DECAY_REST, LAST, FIRST = range(4)


def dot(a, b, dims=(((1,), (0,)), ((), ()))):
    return lax.dot_general(a, b, dims, preferred_element_type=F32)


def call(kernel, name, out_shape, in_specs, args, limit_mib=12, scratch=(), aliases=None, flops=1):
    space = {id(VM): pltpu.VMEM, id(HB): pltpu.HBM}
    args = [
        arg if spec is SM else pltpu.with_memory_space_constraint(arg, space[id(spec)])
        for spec, arg in zip(in_specs, args, strict=True)
    ]
    return pl.pallas_call(
        kernel,
        in_specs=in_specs,
        out_specs=[VM if o.memory_space == pltpu.VMEM else HB for o in out_shape],
        out_shape=out_shape,
        scratch_shapes=scratch,
        input_output_aliases=aliases or {},
        compiler_params=pltpu.CompilerParams(vmem_limit_bytes=limit_mib * 2**20),
        cost_estimate=pl.CostEstimate(flops=int(flops), bytes_accessed=1, transcendentals=0),
        name=name,
    )(*args)


def start(sems, *pairs):
    copies = [
        pltpu.make_async_copy(source, target, sems.at[i]) for i, (source, target) in enumerate(pairs)
    ]
    for copy in copies:
        copy.start()
    return copies


def split(value):
    high = value.astype(BF16)
    return high, (value - high.astype(F32)).astype(BF16)


def silu(gates):
    v = gates.astype(F32)
    return 0.5 * v * (1.0 + jnp.tanh(0.5 * v))


def row_at(rows, k):
    return jnp.sum(jnp.where(iota(rows.shape, 0) == k, rows, 0.0), axis=0, keepdims=True)


def iota(shape, dim):
    return lax.broadcasted_iota(jnp.int32, shape, dim)


def state_kernel(
    heads, blocks, places, x_hbm, b_hbm, c_hbm, ld_hbm, doc_hbm, spread_ref, *rest
):
    crow_ref, entry_ref, exit_ref, local_ref, keep_ref, send_ref, pre_ref, blk_ref, info_ref = rest[:9]
    b_ref, c_ref, padded, running, ld_ref, doc_ref, x_ref, sems = rest[9:]
    n, inner = running.shape
    half = n // 2
    parts = [pl.ds(k * GROUP, GROUP) for k in range(blocks)]
    ld_copy, doc_copy, b_copy, *x_copies, c_copy = start(
        sems, (ld_hbm, ld_ref), (doc_hbm, doc_ref), (b_hbm, b_ref),
        *[(x_hbm.at[p], x_ref.at[p]) for p in parts], (c_hbm, c_ref),
    )
    head_rows = crow_ref.shape[1]
    spread = spread_ref[...]
    later = (iota((GROUP, GROUP), 0) <= iota((GROUP, GROUP), 1)).astype(BF16)
    padded[...] = jnp.zeros_like(padded)
    row = iota((head_rows, GROUP), 0)
    states, ends, cols = [], [], []
    pre_ref[...] = jnp.zeros_like(pre_ref)
    blk_ref[...] = jnp.zeros_like(blk_ref)
    info_ref[...] = jnp.zeros_like(info_ref)
    ld_copy.wait()
    doc_copy.wait()
    for k in range(blocks):
        at = slice(k * GROUP, (k + 1) * GROUP)
        padded[k, 0:heads, :] = ld_ref[:, at] * LOG2E
    steps = jnp.concatenate([padded[k, 0:head_rows, :] for k in range(blocks)], axis=0)
    high, rest = split(steps)
    mid, low = split(steps - high.astype(F32))
    cum = dot(high, later) + (dot(mid, later) + dot(low, later))
    for k in range(blocks):
        at = slice(k * GROUP, (k + 1) * GROUP)
        own_cum = cum[k * head_rows : (k + 1) * head_rows]
        own_cum = jnp.where(row == head_rows - 1, doc_ref[:, at].astype(F32), own_cum)
        crow_ref[k] = own_cum
        padded[k, 0:head_rows, :] = own_cum
    b_copy.wait()
    for k in range(blocks):
        at = slice(k * GROUP, (k + 1) * GROUP)
        ccol = padded[k].T
        cols.append(ccol)
        docs = ccol[:, head_rows - 1 : head_rows]
        end = ccol[GROUP - 1 :]
        ends.append(end)
        end_doc = end[:, head_rows - 1 : head_rows]
        exit_w = jnp.where(docs == end_doc, jnp.exp2(jnp.minimum(end - ccol, 0.0)), 0.0).astype(BF16)
        exit_ref[at, :] = exit_w
        x_copies[k].wait()
        scaled = (dot(exit_w, spread) * x_ref[at, :].astype(F32)).astype(BF16)
        states.append(dot(b_ref[at, :], scaled, TN))
    doc_of = lambda line: line[:, head_rows - 1 : head_rows]
    first_doc = doc_of(cols[0][0:1])
    priors = [first_doc] + [doc_of(end) for end in ends[:-1]]
    last_doc = doc_of(ends[-1])
    total = jnp.zeros_like(ends[0])
    decays, prefixes = [], []
    for end, prior in zip(ends, priors):
        decays.append(jnp.where(doc_of(end) == prior, jnp.exp2(end), 0.0))
        total = total + end
        prefixes.append(jnp.where(doc_of(end) == first_doc, jnp.exp2(total), 0.0))
    stacked = decays + prefixes + [jnp.exp2(total)]
    stacked.append(jnp.zeros((-len(stacked) % 8, LANES), F32))
    high, rest = split(jnp.concatenate(stacked, axis=0))
    wide = dot(high, spread) + dot(rest, spread)
    blk_ref[0:blocks, :] = wide[0:blocks]
    pre_ref[0:1, :] = jnp.ones((1, inner), F32)
    pre_ref[1:blocks, :] = wide[blocks : 2 * blocks - 1]
    local_ref[0] = jnp.zeros((n, inner), BF16)
    now = states[0]
    for k in range(1, blocks):
        local_ref[k] = now.astype(BF16)
        now = wide[k : k + 1] * now + states[k]
    running[...] = now
    raw = wide[2 * blocks : 2 * blocks + 1]
    last_row = jnp.broadcast_to(last_doc + 1.0, (1, inner))
    first_row = jnp.broadcast_to(first_doc + 1.0, (1, inner))
    info_ref[0:1, :] = raw
    info_ref[1:2, :] = last_row
    info_ref[2:3, :] = first_row
    side = places[0]
    keep_ref[...] = running[pl.ds(pl.multiple_of(side * half, half), half), :].astype(BF16)
    send_ref[0:half, :] = running[pl.ds(pl.multiple_of((1 - side) * half, half), half), :].astype(BF16)
    send_ref[half:, :] = tags(raw, last_row, first_row)
    for k, prior in enumerate(priors):
        at = slice(k * GROUP, (k + 1) * GROUP)
        same = doc_of(cols[k]) == prior
        entry_ref[at, :] = jnp.where(same, jnp.exp2(jnp.minimum(cols[k], 0.0)), 0.0).astype(BF16)
    c_copy.wait()


def tags(decay, last, first):
    high, rest = split(decay)
    rows = [high.astype(F32), rest.astype(F32), last, first]
    rows.append(jnp.zeros((TILE - len(rows), decay.shape[1]), F32))
    return jnp.concatenate(rows, axis=0).astype(BF16)


def untagged(block):
    half = block.shape[0] - TILE
    state, rows = block[:half].astype(F32), block[half:].astype(F32)
    row = lambda i: rows[i : i + 1]
    return state, row(DECAY) + row(DECAY_REST), row(LAST), row(FIRST)


def local_states(places, inputs, write_keys, read_keys, log_decay, docs_row, spread):
    tokens, inner = inputs.shape
    heads = log_decay.shape[0]
    n = write_keys.shape[1]
    blocks = tokens // GROUP
    head_rows = -(-(heads + 1) // 8) * 8
    block_rows = -(-blocks // 8) * 8
    return call(
        functools.partial(state_kernel, heads, blocks),
        "local_states",
        [
            pltpu.VMEM((blocks, head_rows, GROUP), F32),
            pltpu.VMEM((tokens, LANES), BF16),
            pltpu.VMEM((tokens, LANES), BF16),
            pltpu.VMEM((blocks, n, inner), BF16),
            pltpu.VMEM((n // 2, inner), BF16),
            pltpu.VMEM((n // 2 + TILE, inner), BF16),
            pltpu.VMEM((block_rows, inner), F32),
            pltpu.VMEM((block_rows, inner), F32),
            pltpu.VMEM((8, inner), F32),
            pltpu.VMEM((tokens, n), BF16),
            pltpu.VMEM((tokens, n), BF16),
        ],
        [SM] + [HB] * 5 + [VM],
        (places, inputs, write_keys, read_keys, log_decay, docs_row, spread),
        scratch=[
            pltpu.VMEM((blocks, LANES, GROUP), F32),
            pltpu.VMEM((n, inner), F32),
            pltpu.VMEM((heads, tokens), F32),
            pltpu.VMEM((1, tokens), jnp.int32),
            pltpu.VMEM((tokens, inner), BF16),
            pltpu.SemaphoreType.DMA((4 + blocks,)),
        ],
    )


def inside_kernel(
    heads, width, blocks, backward, fetched, chips, which, places,
    x_ref, b_ref, c_ref, crow_ref, skip_ref, _, *rest
):
    per_chip = blocks // chips
    if backward and which[0]:
        rest = rest[1:]
    fetch_hbm, out_ref, fetch_vm, padded = (
        rest[:fetched], rest[fetched], rest[fetched + 1 : 2 * fetched + 1], rest[2 * fetched + 1]
    )
    half = GROUP // 2
    head_rows = crow_ref.shape[1]
    per = LANES // width
    part = lambda k: pl.ds(pl.multiple_of(k * GROUP, GROUP), GROUP)
    if not backward:
        x_sems, x_hbm, x_ref = rest[-2], x_ref, rest[-1]
        incoming = lambda k: pltpu.make_async_copy(x_hbm.at[part(k)], x_ref.at[part(k)], x_sems.at[k])
        for k in range(blocks):
            incoming(k).start()
    copies = start(rest[2 * fetched + 2], *zip(fetch_hbm, fetch_vm)) if fetched else []
    lane = iota((GROUP, LANES), 1)
    rows, cols = iota((GROUP, GROUP), 0), iota((GROUP, GROUP), 1)
    causal = (rows <= cols) if backward else (cols <= rows)
    padded[...] = jnp.zeros_like(padded)

    @pl.loop(which[0] * per_chip, which[1] * per_chip)
    def _(step):
        k = step
        if backward:
            turn = places[1] // 2 + step // per_chip
            k = lax.rem(turn, chips) * per_chip + lax.rem(step, per_chip)
        at = part(k)
        padded[0:head_rows, :] = crow_ref[k]
        col = padded[...].T
        docs_row = crow_ref[k, head_rows - 1 : head_rows, :]
        allowed = (col[:, head_rows - 1 : head_rows] == docs_row) & causal
        if backward:
            scores = dot(b_ref[at, :], c_ref[at, :], NT)
        else:
            scores = dot(c_ref[at, :], b_ref[at, :], NT)
        scores = jnp.where(allowed, scores, 0.0)
        if not backward:
            incoming(k).wait()
        for j in range(heads // per):
            cut = slice(j * LANES, (j + 1) * LANES)
            x = x_ref[at, cut]
            base = skip_ref[:, cut] * x.astype(F32)
            top, bottom = base[:half], base[half:]
            for i in range(per):
                h = j * per + i
                own = jnp.where(lane // width == i, x, jnp.zeros_like(x))
                at_row = crow_ref[k, h : h + 1, :]
                at_col = col[:, h : h + 1]

                def weights(r, c):
                    if backward:
                        gap = at_row[:, c] - at_col[r]
                    else:
                        gap = at_col[r] - at_row[:, c]
                    return (jnp.exp2(jnp.minimum(gap, 0.0)) * scores[r, c]).astype(BF16)

                low, high, both = slice(0, half), slice(half, GROUP), slice(0, GROUP)
                if backward:
                    top = top + dot(weights(low, both), own)
                    bottom = bottom + dot(weights(high, high), own[half:])
                else:
                    top = top + dot(weights(low, low), own[:half])
                    bottom = bottom + dot(weights(high, both), own)
            low_at = pl.ds(pl.multiple_of(k * GROUP, GROUP), half)
            high_at = pl.ds(pl.multiple_of(k * GROUP + half, half), half)
            out_ref[low_at, cut] = top.astype(BF16)
            out_ref[high_at, cut] = bottom.astype(BF16)

    for copy in copies:
        copy.wait()


def inside(places, x, write_keys, read_keys, crow, skip, heads, after, fetch=(), which=None, earlier=None):
    tokens, inner = x.shape
    blocks = tokens // GROUP
    backward = which is not None
    chips = lax.axis_size("head") // 2 if backward else 1
    carried = [] if earlier is None else [earlier]
    return call(
        functools.partial(
            inside_kernel, heads, inner // heads, blocks, backward, len(fetch), chips, which or (0, 1)
        ),
        "inside_backward" if backward else "inside_forward",
        [pltpu.VMEM((tokens, inner), BF16)] + [pltpu.VMEM(a.shape, a.dtype) for a in fetch],
        [SM] + [VM if backward else HB] + [VM] * (5 + len(carried)) + [HB] * len(fetch),
        (places, x, write_keys, read_keys, crow, skip, after, *carried, *fetch),
        scratch=[pltpu.VMEM((LANES, GROUP), F32)]
        + ([pltpu.SemaphoreType.DMA((len(fetch),))] if fetch else [])
        + ([] if backward else [
            pltpu.SemaphoreType.DMA((blocks,)),
            pltpu.VMEM((tokens, inner), BF16),
        ]),
        aliases={7: 0} if carried else None,
    )


def tiling(size):
    step = next(step for step in (512, 256, LANES, size) if size % step == 0)
    return [pl.ds(j * step, step) for j in range(size // step)]


def gate_kernel(
    items, chunk, places, mixed_ref, gates_ref, read_ref, entry_ref, local_ref,
    keep_ref, other_ref, pre_ref, spread_ref, *rest
):
    outs = rest[-len(items) :]
    at_low = places[0] == 0
    keep, other = keep_ref[...].astype(F32), other_ref[...].astype(F32)
    state = jnp.concatenate(
        [jnp.where(at_low, keep, other), jnp.where(at_low, other, keep)], axis=0
    )
    for item, out_ref in zip(items, outs):
        at = pl.ds(pl.multiple_of(places[item] * chunk, chunk), chunk)
        k = places[item] * chunk // GROUP
        entering = (local_ref[k].astype(F32) + row_at(pre_ref[...], k) * state).astype(BF16)
        carried = dot(read_ref[at, :], entering) * dot(entry_ref[at, :], spread_ref[...])
        out_ref[...] = (
            (mixed_ref[at, :].astype(F32) + carried) * silu(gates_ref[at, :])
        ).astype(BF16)


def gated_chunks(
    chunk, items, places, mixed, gates, read_keys, entry, local, keep, other, pre, spread, after
):
    inner = mixed.shape[1]
    return call(
        functools.partial(gate_kernel, items, chunk),
        "gated_chunks",
        [pltpu.VMEM((chunk, inner), BF16)] * len(items),
        [SM] + [VM] * (9 + len(after)),
        (places, mixed, gates, read_keys, entry, local, keep, other, pre, spread, *after),
    )


def project_kernel(has_part, count, gated_ref, w_ref, *rest):
    outs = rest[-count:]
    width = outs[0].shape[1]
    for i, out_ref in enumerate(outs):
        for cut in tiling(width):
            at = pl.ds(i * width + cut.start, cut.size)
            total = dot(gated_ref[...], w_ref[:, at])
            if has_part:
                total = rest[0][:, at] + total
            out_ref[:, cut] = total.astype(out_ref.dtype)


def project(gated, weight, part, kind, after=(), count=1, flops=1):
    shape = (gated.shape[0], weight.shape[1] // count)
    parts = [] if part is None else [part]
    return call(
        functools.partial(project_kernel, bool(parts), count),
        "project",
        [pltpu.VMEM(shape, kind)] * count,
        [VM] * (2 + len(parts) + len(after)),
        (gated, weight, *parts, *after),
        flops=flops,
    )


def sum_kernel(own_ref, *rest):
    landed_refs, (out_hbm, out_ref, sems) = rest[:-3], rest[-3:]
    outgoing = []
    width = landed_refs[0].shape[1] if landed_refs else own_ref.shape[1]
    for i in range(own_ref.shape[1] // width):
        at = pl.ds(i * width, width)
        total = own_ref[:, at]
        for ref in landed_refs[i :: own_ref.shape[1] // width]:
            total = total + ref[...].astype(F32)
        out_ref[:, at] = total.astype(BF16)
        outgoing += start(sems.at[i], (out_ref.at[:, at], out_hbm.at[:, at]))
    for copy in outgoing:
        copy.wait()


def chunk_sum(own, landed):
    return call(
        sum_kernel,
        "chunk_sum",
        [pltpu.HBM(own.shape, BF16)],
        [VM] * (1 + len(landed)),
        (own, *landed),
        scratch=[
            pltpu.VMEM(own.shape, BF16),
            pltpu.SemaphoreType.DMA((HALVES, 1)),
        ],
    )[0]


def grad_kernel(items, chunk, first, final, distant, places, *refs):
    count = len(items)
    go_refs, refs = refs[:count], refs[count:]
    if distant:
        go_ref, sems, refs = refs[-2], refs[-1], refs[:-2]
        for copy in start(sems, (go_refs[0], go_ref)):
            copy.wait()
        go_refs = [go_ref]
    gates_ref, read_ref, entry_ref, pre_ref, spread_ref, w_ref, _ = refs[:7]
    refs = refs[7:]
    if not first:
        sum_in, refs = refs[0], refs[3:]
    mix_ref, states_ref = refs[:2]
    summed = None if first else sum_in[...]
    for i, item in enumerate(items):
        at = pl.ds(pl.multiple_of(places[item] * chunk, chunk), chunk)
        k = places[item] * chunk // GROUP
        for cut in tiling(w_ref.shape[0]):
            grad = dot(go_refs[i][...], w_ref[cut, :], NT)
            mix_ref[at, cut] = (grad * silu(gates_ref[at, cut])).astype(BF16)
        scaled = (dot(entry_ref[at, :], spread_ref[...]) * mix_ref[at, :].astype(F32)).astype(BF16)
        state = dot(read_ref[at, :], scaled, TN)
        states_ref[places[item]] = state.astype(BF16)
        part = row_at(pre_ref[...], k) * state
        summed = part if summed is None else summed + part
    if final:
        half = summed.shape[0] // 2
        at_low = places[0] == 0
        refs[2][...] = jnp.where(at_low, summed[:half], summed[half:]).astype(BF16)
        refs[3][...] = jnp.where(at_low, summed[half:], summed[:half]).astype(BF16)
    else:
        refs[2][...] = summed


def grad_chunks(
    chunk, items, places, arrived, gates, read_keys, entry, pre, spread, out_weight, earlier, final, after,
    distant=False,
):
    count = len(arrived)
    inner = out_weight.shape[0]
    tokens = gates.shape[0]
    n = read_keys.shape[1]
    first = earlier is None
    out_shape = [pltpu.VMEM((tokens, inner), BF16), pltpu.VMEM((tokens // chunk, n, inner), BF16)]
    out_shape += [pltpu.VMEM((n // 2, inner), BF16)] * 2 if final else [pltpu.VMEM((n, inner), F32)]
    at = 1 + count + 7
    return call(
        functools.partial(grad_kernel, items, chunk, first, final, distant),
        "grad_chunks",
        out_shape,
        [SM] + [HB if distant else VM] * count + [VM] * (7 + (0 if first else 3)),
        (
            places, *arrived, gates, read_keys, entry, pre, spread, out_weight, after,
            *([] if first else (earlier[2], earlier[0], earlier[1])),
        ),
        scratch=[pltpu.VMEM(arrived[0].shape, BF16), pltpu.SemaphoreType.DMA((1,))] if distant else (),
        aliases=None if first else {at + 1: 0, at + 2: 1},
    )


def back_kernel(
    blocks, places, part_ref, b_ref, exit_ref, states_ref, blk_ref, keep_ref, other_ref, spread_ref,
    out_hbm, running, out_ref, out_sems,
):
    half = keep_ref.shape[0]
    per = states_ref.shape[0] // blocks
    side = places[0]
    running[pl.ds(pl.multiple_of(side * half, half), half), :] = keep_ref[...].astype(F32)
    running[pl.ds(pl.multiple_of((1 - side) * half, half), half), :] = other_ref[...].astype(F32)
    outgoing = []
    for k in reversed(range(blocks)):
        at = pl.ds(k * GROUP, GROUP)
        carried = dot(b_ref[at, :], running[...].astype(BF16)) * dot(exit_ref[at, :], spread_ref[...])
        out_ref[at, :] = (part_ref[at, :].astype(F32) + carried).astype(BF16)
        outgoing += start(out_sems.at[k], (out_ref.at[at], out_hbm.at[at]))
        if k:
            state = states_ref[k * per].astype(F32)
            for i in range(1, per):
                state = state + states_ref[k * per + i].astype(F32)
            running[...] = state + blk_ref[k : k + 1, :] * running[...]
    for copy in outgoing:
        copy.wait()


def back_tail(places, part, write_keys, exit_w, states, blk, keep, other, spread):
    tokens, inner = part.shape
    n = write_keys.shape[1]
    blocks = tokens // GROUP
    return call(
        functools.partial(back_kernel, blocks),
        "back_tail",
        [pltpu.HBM((tokens, inner), BF16)],
        [SM] + [VM] * 8,
        (places, part, write_keys, exit_w, states, blk, keep, other, spread),
        flops=TAIL_COST,
        scratch=[
            pltpu.VMEM((n, inner), F32),
            pltpu.VMEM((tokens, inner), BF16),
            pltpu.SemaphoreType.DMA((blocks, 1)),
        ],
    )[0]


def shifted(block, axis, distance):
    size = lax.axis_size(axis)
    route = [(i, i + distance) for i in range(size) if 0 <= i + distance < size]
    return lax.ppermute(block, axis, route)


def swapped(block, axis):
    return lax.ppermute(block, axis, [(i, i ^ 1) for i in range(lax.axis_size(axis))])


def rotated(block, axis, distance):
    size = lax.axis_size(axis)
    return lax.ppermute(block, axis, [(i, (i + distance) % size) for i in range(size)])


def pair_kernel(places, keep_ref, got_ref, info_ref, _, tagged_ref, near_ref, facts_ref):
    low = places[0] == 0
    pick = lambda own, mate: (jnp.where(low, own, mate), jnp.where(low, mate, own))
    got, mate_raw, mate_last, mate_first = untagged(got_ref[...])
    near, far = pick(keep_ref[...].astype(F32), got)
    near_raw, far_raw = pick(info_ref[0:1, :], mate_raw)
    near_last, far_last = pick(info_ref[1:2, :], mate_last)
    near_first, far_first = pick(info_ref[2:3, :], mate_first)
    far_live = (far_first == near_last).astype(F32)
    far_decay = jnp.where(far_last == far_first, far_raw, 0.0) * far_live
    near_decay = jnp.where(near_last == near_first, near_raw, 0.0)
    half = near.shape[0]
    tagged_ref[:half, :] = (far + far_decay * near).astype(BF16)
    tagged_ref[half:, :] = tags(far_decay * near_decay, far_last, near_first)
    near_ref[...] = near.astype(BF16)
    facts_ref[...] = jnp.concatenate(
        [near_decay, far_decay, far_live, near_first, jnp.zeros((4, near.shape[1]), F32)], axis=0
    )


def enter_kernel(through, places, near_ref, facts_ref, one_ref, two_ref, _, *rest):
    copies = []
    for i in range(through):
        source, target = rest[i], rest[through + 3 + i]
        step = source.shape[0] // PARTS
        parts = [pl.ds(j * step, step) for j in range(PARTS)]
        copies += start(rest[-1].at[i], *[(source.at[p], target.at[p]) for p in parts])
    mine_ref, hers_ref, out_ref = rest[through : through + 3]
    low = places[0] == 0
    one, one_decay, one_last, one_first = untagged(one_ref[...])
    two, _, two_last, _ = untagged(two_ref[...])
    two = jnp.where(places[places.shape[0] - 2] > 0, two, 0.0)
    facts = facts_ref[...]
    at_near = one + jnp.where(one_first == two_last, one_decay, 0.0) * two
    near_live = (facts[3:4] == one_last).astype(F32)
    near_decay, far_decay, far_live = facts[0:1] * near_live, facts[1:2], facts[2:3]
    at_far = (near_ref[...].astype(F32) + near_decay * at_near) * far_live
    at_near = at_near * near_live
    mine_ref[...] = jnp.where(low, at_near, at_far).astype(BF16)
    hers_ref[...] = jnp.where(low, at_far, at_near).astype(BF16)
    out_ref[...] = jnp.concatenate(
        [near_decay, far_decay, near_live, far_live, jnp.zeros((4, near_decay.shape[1]), F32)], axis=0
    )
    for copy in copies:
        copy.wait()


def pair_back_kernel(places, keep_ref, got_ref, facts_ref, _, tagged_ref, near_ref):
    low = places[0] == 0
    facts = facts_ref[...]
    keep, got = keep_ref[...].astype(F32), got_ref[...].astype(F32)
    near = jnp.where(low, got, keep) * facts[3:4]
    far = jnp.where(low, keep, got) * facts[2:3]
    half = near.shape[0]
    one = jnp.ones_like(facts[0:1])
    tagged_ref[:half, :] = (far + facts[0:1] * near).astype(BF16)
    tagged_ref[half:, :] = tags(facts[0:1] * facts[1:2], one, one)
    near_ref[...] = near.astype(BF16)


def enter_back_kernel(places, near_ref, facts_ref, one_ref, two_ref, _, mine_ref, hers_ref):
    low = places[0] == 0
    one, one_decay, one_last, one_first = untagged(one_ref[...])
    two, _, two_last, _ = untagged(two_ref[...])
    two = jnp.where(places[places.shape[0] - 1] > 0, two, 0.0)
    at_near = one + jnp.where(one_first == two_last, one_decay, 0.0) * two
    at_far = near_ref[...].astype(F32) + facts_ref[1:2, :] * at_near
    mine_ref[...] = jnp.where(low, at_far, at_near).astype(BF16)
    hers_ref[...] = jnp.where(low, at_near, at_far).astype(BF16)


def small(kernel, name, shapes, args, after, through=()):
    out_shape = [pltpu.VMEM(dims, kind) for dims, kind in shapes]
    out_shape += [pltpu.VMEM(a.shape, a.dtype) for a in through]
    return call(
        kernel, name, out_shape, [SM] + [VM] * len(args) + [HB] * len(through), (*args, after, *through),
        scratch=[pltpu.SemaphoreType.DMA((len(through), PARTS))] if through else (),
    )


def between_pairs(tagged, way):
    half = tagged.shape[0] - TILE
    window = max(lax.axis_size("seq") // 4, 1)
    if window <= 2:
        two = rotated(tagged, "seq", 4 * way) if window == 2 else jnp.zeros_like(tagged)
        return shifted(tagged, "seq", 2 * way), two
    total, decay, _, first = untagged(tagged)
    came, _, came_last, _ = untagged(shifted(tagged, "seq", 2 * way))
    decay = jnp.where(first == came_last, decay, 0.0)
    total = (total + decay * came).astype(BF16)
    reach = 2
    while reach < window:
        decay = decay * shifted(decay, "seq", way * reach)
        total = (total.astype(F32) + decay * shifted(total, "seq", 2 * way * reach).astype(F32)).astype(BF16)
        reach *= 2
    one = shifted(jnp.concatenate([total, tagged[half:]], axis=0), "seq", 2 * way)
    return one, jnp.zeros_like(one)


def shards(
    inputs, gates, write_keys, read_keys, log_decay, skip_gain, doc_ids, out_weight, grad_out
):
    tokens, inner = inputs.shape
    heads = log_decay.shape[0]
    width = inner // heads
    members = lax.axis_size("head")
    chips = members // 2
    chunk = tokens // members
    here = lax.axis_index("head")
    chip, core = here // 2, here % 2
    mate = here ^ 1
    side = lax.axis_index("seq") % 2
    numbers = [here, mate]
    for d in range(1, chips):
        source = (here - 2 * d) % members
        target = ((chip + d) % chips) * 2
        numbers += [source, source ^ 1, target + 1 - core, target + core]
    pair_at, pairs = lax.axis_index("seq") // 2, lax.axis_size("seq") // 2
    places = jnp.stack([side] + numbers + [pair_at >= 2, pair_at + 2 < pairs]).astype(jnp.int32)

    remote = [rotated(grad_out, "head", 2 * d) for d in range(1, chips)]
    sibling = swapped(grad_out, "head")
    mate_weight = swapped(out_weight, "head")

    spread = (
        jnp.arange(LANES)[:, None] == (jnp.arange(inner) // width)[None, :]
    ).astype(BF16)
    skip = jnp.repeat(skip_gain, width)[None, :]
    crow, entry, exit_w, local, keep, send, pre, blk, info, b, c = local_states(
        places, inputs, write_keys, read_keys, log_decay, doc_ids[None, :], spread
    )
    half, tagged, facts_shape = keep.shape, send.shape, info.shape
    mixed, gates, weight, own_grad = inside(
        places, inputs, b, c, crow, skip, heads, send, (gates, out_weight, grad_out)
    )
    pair, near, facts = small(
        pair_kernel, "pair", [(tagged, BF16), (half, BF16), (facts_shape, F32)],
        (places, keep, swapped(send, "seq"), info), mixed,
    )
    one, two = between_pairs(pair, 1)

    def grads(items, arrived, earlier, final, after, distant=False):
        return grad_chunks(
            chunk, items, places, arrived, gates, c, entry, pre, spread, weight, earlier, final, after,
            distant,
        )

    back = grads((1, 2), [own_grad, sibling], None, chips == 1, pair)
    part, mate_weight = inside(
        places, back[0], b, c, crow, skip, heads, back[1], (mate_weight,), which=(0, 1)
    )
    enter_keep, hers, facts, *remote = small(
        functools.partial(enter_kernel, len(remote)), "enter", [(half, BF16), (half, BF16), (facts_shape, F32)],
        (places, near, facts, one, two), part, remote,
    )
    enter_other = swapped(hers, "seq")

    def gated(items, *after):
        return gated_chunks(
            chunk, items, places, mixed, gates, c, entry, local, enter_keep, enter_other, pre, spread, after
        )

    for d in range(chips - 1):
        relayed = swapped(remote[d], "head")
        back = grads((3 + 4 * d,), [remote[d]], back, False, hers)
        back = grads((4 + 4 * d,), [relayed], back, d == chips - 2, back[1])
    mix, states, back_keep, back_send = back
    got = swapped(back_send, "seq")
    after, landed = back_send, []
    for d in range(chips - 1):
        give, stay = gated((5 + 4 * d, 6 + 4 * d), after)
        (after,) = project(stay, weight, None, F32, (give,), flops=FAR_COST)
        for total in project(swapped(give, "head"), mate_weight, after, BF16, count=HALVES):
            landed.append(rotated(total, "head", 2 * (d + 1)))
            after = total
    pair, near = small(
        pair_back_kernel, "pair_back", [(tagged, BF16), (half, BF16)],
        (places, back_keep, got, facts), after,
    )
    one, two = between_pairs(pair, -1)
    give, stay = gated((2, 1), pair)
    (own,) = project(stay, weight, None, F32, (give,), flops=NEAR_COST)
    (own,) = project(swapped(give, "head"), mate_weight, own, F32)
    part = inside(places, mix, b, c, crow, skip, heads, own, which=(1, chips), earlier=part)[0]
    arrive_keep, hers = small(
        enter_back_kernel, "enter_back", [(half, BF16), (half, BF16)],
        (places, near, facts, one, two), part,
    )
    arrive_other = swapped(hers, "seq")
    out = chunk_sum(own, landed)
    grad_inputs = back_tail(
        places, part, b, exit_w, states, blk, arrive_keep, arrive_other, spread
    )
    return out, grad_inputs


def solution(mesh):
    in_specs = (
        P("seq", "head"),
        P("seq", "head"),
        P("seq", None),
        P("seq", None),
        P("head", "seq"),
        P("head"),
        P("seq"),
        P("head", None),
        P(("seq", "head"), None),
    )
    out_specs = (P(("seq", "head"), None), P("seq", "head"))
    return jax.shard_map(shards, mesh=mesh, in_specs=in_specs, out_specs=out_specs, check_vma=False)
```

```python
import functools
import math

import jax
import jax.numpy as jnp
from jax import lax
from jax.experimental import pallas as pl
from jax.experimental.pallas import tpu as pltpu
from jax.sharding import PartitionSpec as P

GROUP = 256
LANES = 128
TILE = 16
PARTS = 4
TAIL_COST, FAR_COST, NEAR_COST = 1.73e9, 2.306e10, 9.224e9
LOG2E = math.log2(math.e)
F32 = jnp.float32
BF16 = jnp.bfloat16
NT = (((1,), (1,)), ((), ()))
TN = (((0,), (0,)), ((), ()))
VM = pl.BlockSpec(memory_space=pltpu.VMEM)
SM = pl.BlockSpec(memory_space=pltpu.SMEM)
HB = pl.BlockSpec(memory_space=pltpu.HBM)
DECAY, DECAY_REST, LAST, FIRST = range(4)


def dot(a, b, dims=(((1,), (0,)), ((), ()))):
    return lax.dot_general(a, b, dims, preferred_element_type=F32)


def call(kernel, name, out_shape, in_specs, args, limit_mib=12, scratch=(), aliases=None, flops=1):
    space = {id(VM): pltpu.VMEM, id(HB): pltpu.HBM}
    args = [
        arg if spec is SM else pltpu.with_memory_space_constraint(arg, space[id(spec)])
        for spec, arg in zip(in_specs, args, strict=True)
    ]
    return pl.pallas_call(
        kernel,
        in_specs=in_specs,
        out_specs=[VM if o.memory_space == pltpu.VMEM else HB for o in out_shape],
        out_shape=out_shape,
        scratch_shapes=scratch,
        input_output_aliases=aliases or {},
        compiler_params=pltpu.CompilerParams(vmem_limit_bytes=limit_mib * 2**20),
        cost_estimate=pl.CostEstimate(flops=int(flops), bytes_accessed=1, transcendentals=0),
        name=name,
    )(*args)


def start(sems, *pairs):
    copies = [
        pltpu.make_async_copy(source, target, sems.at[i]) for i, (source, target) in enumerate(pairs)
    ]
    for copy in copies:
        copy.start()
    return copies


def split(value):
    high = value.astype(BF16)
    return high, (value - high.astype(F32)).astype(BF16)


def silu(gates):
    v = gates.astype(F32)
    return 0.5 * v * (1.0 + jnp.tanh(0.5 * v))


def row_at(rows, k):
    return jnp.sum(jnp.where(iota(rows.shape, 0) == k, rows, 0.0), axis=0, keepdims=True)


def iota(shape, dim):
    return lax.broadcasted_iota(jnp.int32, shape, dim)


def state_kernel(
    heads, blocks, places, x_hbm, b_hbm, c_hbm, ld_hbm, doc_hbm, spread_ref, *rest
):
    crow_ref, entry_ref, exit_ref, local_ref, keep_ref, send_ref, pre_ref, blk_ref, info_ref = rest[:9]
    b_ref, c_ref, padded, running, ld_ref, doc_ref, x_ref, sems = rest[9:]
    n, inner = running.shape
    half = n // 2
    parts = [pl.ds(k * GROUP, GROUP) for k in range(blocks)]
    ld_copy, doc_copy, b_copy, *x_copies, c_copy = start(
        sems, (ld_hbm, ld_ref), (doc_hbm, doc_ref), (b_hbm, b_ref),
        *[(x_hbm.at[p], x_ref.at[p]) for p in parts], (c_hbm, c_ref),
    )
    head_rows = crow_ref.shape[1]
    spread = spread_ref[...]
    later = (iota((GROUP, GROUP), 0) <= iota((GROUP, GROUP), 1)).astype(BF16)
    padded[...] = jnp.zeros_like(padded)
    row = iota((head_rows, GROUP), 0)
    states, ends, cols = [], [], []
    pre_ref[...] = jnp.zeros_like(pre_ref)
    blk_ref[...] = jnp.zeros_like(blk_ref)
    info_ref[...] = jnp.zeros_like(info_ref)
    ld_copy.wait()
    doc_copy.wait()
    for k in range(blocks):
        at = slice(k * GROUP, (k + 1) * GROUP)
        padded[k, 0:heads, :] = ld_ref[:, at] * LOG2E
    steps = jnp.concatenate([padded[k, 0:head_rows, :] for k in range(blocks)], axis=0)
    high, rest = split(steps)
    mid, low = split(steps - high.astype(F32))
    cum = dot(high, later) + (dot(mid, later) + dot(low, later))
    for k in range(blocks):
        at = slice(k * GROUP, (k + 1) * GROUP)
        own_cum = cum[k * head_rows : (k + 1) * head_rows]
        own_cum = jnp.where(row == head_rows - 1, doc_ref[:, at].astype(F32), own_cum)
        crow_ref[k] = own_cum
        padded[k, 0:head_rows, :] = own_cum
    b_copy.wait()
    for k in range(blocks):
        at = slice(k * GROUP, (k + 1) * GROUP)
        ccol = padded[k].T
        cols.append(ccol)
        docs = ccol[:, head_rows - 1 : head_rows]
        end = ccol[GROUP - 1 :]
        ends.append(end)
        end_doc = end[:, head_rows - 1 : head_rows]
        exit_w = jnp.where(docs == end_doc, jnp.exp2(jnp.minimum(end - ccol, 0.0)), 0.0).astype(BF16)
        exit_ref[at, :] = exit_w
        x_copies[k].wait()
        scaled = (dot(exit_w, spread) * x_ref[at, :].astype(F32)).astype(BF16)
        states.append(dot(b_ref[at, :], scaled, TN))
    doc_of = lambda line: line[:, head_rows - 1 : head_rows]
    first_doc = doc_of(cols[0][0:1])
    priors = [first_doc] + [doc_of(end) for end in ends[:-1]]
    last_doc = doc_of(ends[-1])
    total = jnp.zeros_like(ends[0])
    decays, prefixes = [], []
    for end, prior in zip(ends, priors):
        decays.append(jnp.where(doc_of(end) == prior, jnp.exp2(end), 0.0))
        total = total + end
        prefixes.append(jnp.where(doc_of(end) == first_doc, jnp.exp2(total), 0.0))
    stacked = decays + prefixes + [jnp.exp2(total)]
    stacked.append(jnp.zeros((-len(stacked) % 8, LANES), F32))
    high, rest = split(jnp.concatenate(stacked, axis=0))
    wide = dot(high, spread) + dot(rest, spread)
    blk_ref[0:blocks, :] = wide[0:blocks]
    pre_ref[0:1, :] = jnp.ones((1, inner), F32)
    pre_ref[1:blocks, :] = wide[blocks : 2 * blocks - 1]
    local_ref[0] = jnp.zeros((n, inner), BF16)
    now = states[0]
    for k in range(1, blocks):
        local_ref[k] = now.astype(BF16)
        now = wide[k : k + 1] * now + states[k]
    running[...] = now
    raw = wide[2 * blocks : 2 * blocks + 1]
    last_row = jnp.broadcast_to(last_doc + 1.0, (1, inner))
    first_row = jnp.broadcast_to(first_doc + 1.0, (1, inner))
    info_ref[0:1, :] = raw
    info_ref[1:2, :] = last_row
    info_ref[2:3, :] = first_row
    side = places[0]
    keep_ref[...] = running[pl.ds(pl.multiple_of(side * half, half), half), :].astype(BF16)
    send_ref[0:half, :] = running[pl.ds(pl.multiple_of((1 - side) * half, half), half), :].astype(BF16)
    send_ref[half:, :] = tags(raw, last_row, first_row)
    for k, prior in enumerate(priors):
        at = slice(k * GROUP, (k + 1) * GROUP)
        same = doc_of(cols[k]) == prior
        entry_ref[at, :] = jnp.where(same, jnp.exp2(jnp.minimum(cols[k], 0.0)), 0.0).astype(BF16)
    c_copy.wait()


def tags(decay, last, first):
    high, rest = split(decay)
    rows = [high.astype(F32), rest.astype(F32), last, first]
    rows.append(jnp.zeros((TILE - len(rows), decay.shape[1]), F32))
    return jnp.concatenate(rows, axis=0).astype(BF16)


def untagged(block):
    half = block.shape[0] - TILE
    state, rows = block[:half].astype(F32), block[half:].astype(F32)
    row = lambda i: rows[i : i + 1]
    return state, row(DECAY) + row(DECAY_REST), row(LAST), row(FIRST)


def local_states(places, inputs, write_keys, read_keys, log_decay, docs_row, spread):
    tokens, inner = inputs.shape
    heads = log_decay.shape[0]
    n = write_keys.shape[1]
    blocks = tokens // GROUP
    head_rows = -(-(heads + 1) // 8) * 8
    block_rows = -(-blocks // 8) * 8
    return call(
        functools.partial(state_kernel, heads, blocks),
        "local_states",
        [
            pltpu.VMEM((blocks, head_rows, GROUP), F32),
            pltpu.VMEM((tokens, LANES), BF16),
            pltpu.VMEM((tokens, LANES), BF16),
            pltpu.VMEM((blocks, n, inner), BF16),
            pltpu.VMEM((n // 2, inner), BF16),
            pltpu.VMEM((n // 2 + TILE, inner), BF16),
            pltpu.VMEM((block_rows, inner), F32),
            pltpu.VMEM((block_rows, inner), F32),
            pltpu.VMEM((8, inner), F32),
            pltpu.VMEM((tokens, n), BF16),
            pltpu.VMEM((tokens, n), BF16),
        ],
        [SM] + [HB] * 5 + [VM],
        (places, inputs, write_keys, read_keys, log_decay, docs_row, spread),
        scratch=[
            pltpu.VMEM((blocks, LANES, GROUP), F32),
            pltpu.VMEM((n, inner), F32),
            pltpu.VMEM((heads, tokens), F32),
            pltpu.VMEM((1, tokens), jnp.int32),
            pltpu.VMEM((tokens, inner), BF16),
            pltpu.SemaphoreType.DMA((4 + blocks,)),
        ],
    )


def inside_kernel(
    heads, width, blocks, backward, fetched, chips, which, places,
    x_ref, b_ref, c_ref, crow_ref, skip_ref, _, *rest
):
    per_chip = blocks // chips
    if backward and which[0]:
        rest = rest[1:]
    fetch_hbm, out_ref, fetch_vm, padded = (
        rest[:fetched], rest[fetched], rest[fetched + 1 : 2 * fetched + 1], rest[2 * fetched + 1]
    )
    half = GROUP // 2
    head_rows = crow_ref.shape[1]
    per = LANES // width
    part = lambda k: pl.ds(pl.multiple_of(k * GROUP, GROUP), GROUP)
    if not backward:
        x_sems, x_hbm, x_ref = rest[-2], x_ref, rest[-1]
        incoming = lambda k: pltpu.make_async_copy(x_hbm.at[part(k)], x_ref.at[part(k)], x_sems.at[k])
        for k in range(blocks):
            incoming(k).start()
    copies = start(rest[2 * fetched + 2], *zip(fetch_hbm, fetch_vm)) if fetched else []
    lane = iota((GROUP, LANES), 1)
    rows, cols = iota((GROUP, GROUP), 0), iota((GROUP, GROUP), 1)
    causal = (rows <= cols) if backward else (cols <= rows)
    padded[...] = jnp.zeros_like(padded)

    @pl.loop(which[0] * per_chip, which[1] * per_chip)
    def _(step):
        k = step
        if backward:
            turn = places[1] // 2 + step // per_chip
            k = lax.rem(turn, chips) * per_chip + lax.rem(step, per_chip)
        at = part(k)
        padded[0:head_rows, :] = crow_ref[k]
        col = padded[...].T
        docs_row = crow_ref[k, head_rows - 1 : head_rows, :]
        allowed = (col[:, head_rows - 1 : head_rows] == docs_row) & causal
        if backward:
            scores = dot(b_ref[at, :], c_ref[at, :], NT)
        else:
            scores = dot(c_ref[at, :], b_ref[at, :], NT)
        scores = jnp.where(allowed, scores, 0.0)
        if not backward:
            incoming(k).wait()
        for j in range(heads // per):
            cut = slice(j * LANES, (j + 1) * LANES)
            x = x_ref[at, cut]
            base = skip_ref[:, cut] * x.astype(F32)
            top, bottom = base[:half], base[half:]
            for i in range(per):
                h = j * per + i
                own = jnp.where(lane // width == i, x, jnp.zeros_like(x))
                at_row = crow_ref[k, h : h + 1, :]
                at_col = col[:, h : h + 1]

                def weights(r, c):
                    if backward:
                        gap = at_row[:, c] - at_col[r]
                    else:
                        gap = at_col[r] - at_row[:, c]
                    return (jnp.exp2(jnp.minimum(gap, 0.0)) * scores[r, c]).astype(BF16)

                low, high, both = slice(0, half), slice(half, GROUP), slice(0, GROUP)
                if backward:
                    top = top + dot(weights(low, both), own)
                    bottom = bottom + dot(weights(high, high), own[half:])
                else:
                    top = top + dot(weights(low, low), own[:half])
                    bottom = bottom + dot(weights(high, both), own)
            low_at = pl.ds(pl.multiple_of(k * GROUP, GROUP), half)
            high_at = pl.ds(pl.multiple_of(k * GROUP + half, half), half)
            out_ref[low_at, cut] = top.astype(BF16)
            out_ref[high_at, cut] = bottom.astype(BF16)

    for copy in copies:
        copy.wait()


def inside(places, x, write_keys, read_keys, crow, skip, heads, after, fetch=(), which=None, earlier=None):
    tokens, inner = x.shape
    blocks = tokens // GROUP
    backward = which is not None
    chips = lax.axis_size("head") // 2 if backward else 1
    carried = [] if earlier is None else [earlier]
    return call(
        functools.partial(
            inside_kernel, heads, inner // heads, blocks, backward, len(fetch), chips, which or (0, 1)
        ),
        "inside_backward" if backward else "inside_forward",
        [pltpu.VMEM((tokens, inner), BF16)] + [pltpu.VMEM(a.shape, a.dtype) for a in fetch],
        [SM] + [VM if backward else HB] + [VM] * (5 + len(carried)) + [HB] * len(fetch),
        (places, x, write_keys, read_keys, crow, skip, after, *carried, *fetch),
        scratch=[pltpu.VMEM((LANES, GROUP), F32)]
        + ([pltpu.SemaphoreType.DMA((len(fetch),))] if fetch else [])
        + ([] if backward else [
            pltpu.SemaphoreType.DMA((blocks,)),
            pltpu.VMEM((tokens, inner), BF16),
        ]),
        aliases={7: 0} if carried else None,
    )


def tiling(size):
    step = next(step for step in (512, 256, LANES, size) if size % step == 0)
    return [pl.ds(j * step, step) for j in range(size // step)]


def gate_kernel(
    items, chunk, places, mixed_ref, gates_ref, read_ref, entry_ref, local_ref,
    keep_ref, other_ref, pre_ref, spread_ref, *rest
):
    outs = rest[-len(items) :]
    at_low = places[0] == 0
    keep, other = keep_ref[...].astype(F32), other_ref[...].astype(F32)
    state = jnp.concatenate(
        [jnp.where(at_low, keep, other), jnp.where(at_low, other, keep)], axis=0
    )
    for item, out_ref in zip(items, outs):
        at = pl.ds(pl.multiple_of(places[item] * chunk, chunk), chunk)
        k = places[item] * chunk // GROUP
        entering = (local_ref[k].astype(F32) + row_at(pre_ref[...], k) * state).astype(BF16)
        carried = dot(read_ref[at, :], entering) * dot(entry_ref[at, :], spread_ref[...])
        out_ref[...] = (
            (mixed_ref[at, :].astype(F32) + carried) * silu(gates_ref[at, :])
        ).astype(BF16)


def gated_chunks(
    chunk, items, places, mixed, gates, read_keys, entry, local, keep, other, pre, spread, after
):
    inner = mixed.shape[1]
    return call(
        functools.partial(gate_kernel, items, chunk),
        "gated_chunks",
        [pltpu.VMEM((chunk, inner), BF16)] * len(items),
        [SM] + [VM] * (9 + len(after)),
        (places, mixed, gates, read_keys, entry, local, keep, other, pre, spread, *after),
    )


def project_kernel(has_part, count, gated_ref, w_ref, *rest):
    outs = rest[-count:]
    width = outs[0].shape[1]
    for i, out_ref in enumerate(outs):
        for cut in tiling(width):
            at = pl.ds(i * width + cut.start, cut.size)
            total = dot(gated_ref[...], w_ref[:, at])
            if has_part:
                total = rest[0][:, at] + total
            out_ref[:, cut] = total.astype(out_ref.dtype)


def project(gated, weight, part, kind, after=(), count=1, flops=1):
    shape = (gated.shape[0], weight.shape[1] // count)
    parts = [] if part is None else [part]
    return call(
        functools.partial(project_kernel, bool(parts), count),
        "project",
        [pltpu.VMEM(shape, kind)] * count,
        [VM] * (2 + len(parts) + len(after)),
        (gated, weight, *parts, *after),
        flops=flops,
    )


def sum_kernel(own_ref, *rest):
    landed_refs, (out_hbm, out_ref, sems) = rest[:-3], rest[-3:]
    outgoing = []
    for j, at in enumerate(tiling(own_ref.shape[1])):
        total = own_ref[:, at]
        for ref in landed_refs:
            total = total + ref[:, at].astype(F32)
        out_ref[:, at] = total.astype(BF16)
        outgoing += start(sems.at[j], (out_ref.at[:, at], out_hbm.at[:, at]))
    for copy in outgoing:
        copy.wait()


def chunk_sum(own, landed):
    return call(
        sum_kernel,
        "chunk_sum",
        [pltpu.HBM(own.shape, BF16)],
        [VM] * (1 + len(landed)),
        (own, *landed),
        scratch=[
            pltpu.VMEM(own.shape, BF16),
            pltpu.SemaphoreType.DMA((len(tiling(own.shape[1])), 1)),
        ],
    )[0]


def grad_kernel(items, chunk, first, final, distant, places, *refs):
    count = len(items)
    go_refs, refs = refs[:count], refs[count:]
    if distant:
        go_ref, sems, refs = refs[-2], refs[-1], refs[:-2]
        for copy in start(sems, (go_refs[0], go_ref)):
            copy.wait()
        go_refs = [go_ref]
    gates_ref, read_ref, entry_ref, pre_ref, spread_ref, w_ref, _ = refs[:7]
    refs = refs[7:]
    if not first:
        sum_in, refs = refs[0], refs[3:]
    mix_ref, states_ref = refs[:2]
    summed = None if first else sum_in[...]
    for i, item in enumerate(items):
        at = pl.ds(pl.multiple_of(places[item] * chunk, chunk), chunk)
        k = places[item] * chunk // GROUP
        for cut in tiling(w_ref.shape[0]):
            grad = dot(go_refs[i][...], w_ref[cut, :], NT)
            mix_ref[at, cut] = (grad * silu(gates_ref[at, cut])).astype(BF16)
        scaled = (dot(entry_ref[at, :], spread_ref[...]) * mix_ref[at, :].astype(F32)).astype(BF16)
        state = dot(read_ref[at, :], scaled, TN)
        states_ref[places[item]] = state.astype(BF16)
        part = row_at(pre_ref[...], k) * state
        summed = part if summed is None else summed + part
    if final:
        half = summed.shape[0] // 2
        at_low = places[0] == 0
        refs[2][...] = jnp.where(at_low, summed[:half], summed[half:]).astype(BF16)
        refs[3][...] = jnp.where(at_low, summed[half:], summed[:half]).astype(BF16)
    else:
        refs[2][...] = summed


def grad_chunks(
    chunk, items, places, arrived, gates, read_keys, entry, pre, spread, out_weight, earlier, final, after,
    distant=False,
):
    count = len(arrived)
    inner = out_weight.shape[0]
    tokens = gates.shape[0]
    n = read_keys.shape[1]
    first = earlier is None
    out_shape = [pltpu.VMEM((tokens, inner), BF16), pltpu.VMEM((tokens // chunk, n, inner), BF16)]
    out_shape += [pltpu.VMEM((n // 2, inner), BF16)] * 2 if final else [pltpu.VMEM((n, inner), F32)]
    at = 1 + count + 7
    return call(
        functools.partial(grad_kernel, items, chunk, first, final, distant),
        "grad_chunks",
        out_shape,
        [SM] + [HB if distant else VM] * count + [VM] * (7 + (0 if first else 3)),
        (
            places, *arrived, gates, read_keys, entry, pre, spread, out_weight, after,
            *([] if first else (earlier[2], earlier[0], earlier[1])),
        ),
        scratch=[pltpu.VMEM(arrived[0].shape, BF16), pltpu.SemaphoreType.DMA((1,))] if distant else (),
        aliases=None if first else {at + 1: 0, at + 2: 1},
    )


def back_kernel(
    blocks, places, part_ref, b_ref, exit_ref, states_ref, blk_ref, keep_ref, other_ref, spread_ref,
    out_hbm, running, out_ref, out_sems,
):
    half = keep_ref.shape[0]
    per = states_ref.shape[0] // blocks
    side = places[0]
    running[pl.ds(pl.multiple_of(side * half, half), half), :] = keep_ref[...].astype(F32)
    running[pl.ds(pl.multiple_of((1 - side) * half, half), half), :] = other_ref[...].astype(F32)
    outgoing = []
    for k in reversed(range(blocks)):
        at = pl.ds(k * GROUP, GROUP)
        carried = dot(b_ref[at, :], running[...].astype(BF16)) * dot(exit_ref[at, :], spread_ref[...])
        out_ref[at, :] = (part_ref[at, :].astype(F32) + carried).astype(BF16)
        outgoing += start(out_sems.at[k], (out_ref.at[at], out_hbm.at[at]))
        if k:
            state = states_ref[k * per].astype(F32)
            for i in range(1, per):
                state = state + states_ref[k * per + i].astype(F32)
            running[...] = state + blk_ref[k : k + 1, :] * running[...]
    for copy in outgoing:
        copy.wait()


def back_tail(places, part, write_keys, exit_w, states, blk, keep, other, spread):
    tokens, inner = part.shape
    n = write_keys.shape[1]
    blocks = tokens // GROUP
    return call(
        functools.partial(back_kernel, blocks),
        "back_tail",
        [pltpu.HBM((tokens, inner), BF16)],
        [SM] + [VM] * 8,
        (places, part, write_keys, exit_w, states, blk, keep, other, spread),
        flops=TAIL_COST,
        scratch=[
            pltpu.VMEM((n, inner), F32),
            pltpu.VMEM((tokens, inner), BF16),
            pltpu.SemaphoreType.DMA((blocks, 1)),
        ],
    )[0]


def shifted(block, axis, distance):
    size = lax.axis_size(axis)
    route = [(i, i + distance) for i in range(size) if 0 <= i + distance < size]
    return lax.ppermute(block, axis, route)


def swapped(block, axis):
    return lax.ppermute(block, axis, [(i, i ^ 1) for i in range(lax.axis_size(axis))])


def rotated(block, axis, distance):
    size = lax.axis_size(axis)
    return lax.ppermute(block, axis, [(i, (i + distance) % size) for i in range(size)])


def pair_kernel(places, keep_ref, got_ref, info_ref, _, tagged_ref, near_ref, facts_ref):
    low = places[0] == 0
    pick = lambda own, mate: (jnp.where(low, own, mate), jnp.where(low, mate, own))
    got, mate_raw, mate_last, mate_first = untagged(got_ref[...])
    near, far = pick(keep_ref[...].astype(F32), got)
    near_raw, far_raw = pick(info_ref[0:1, :], mate_raw)
    near_last, far_last = pick(info_ref[1:2, :], mate_last)
    near_first, far_first = pick(info_ref[2:3, :], mate_first)
    far_live = (far_first == near_last).astype(F32)
    far_decay = jnp.where(far_last == far_first, far_raw, 0.0) * far_live
    near_decay = jnp.where(near_last == near_first, near_raw, 0.0)
    half = near.shape[0]
    tagged_ref[:half, :] = (far + far_decay * near).astype(BF16)
    tagged_ref[half:, :] = tags(far_decay * near_decay, far_last, near_first)
    near_ref[...] = near.astype(BF16)
    facts_ref[...] = jnp.concatenate(
        [near_decay, far_decay, far_live, near_first, jnp.zeros((4, near.shape[1]), F32)], axis=0
    )


def enter_kernel(through, places, near_ref, facts_ref, one_ref, two_ref, _, *rest):
    copies = []
    for i in range(through):
        source, target = rest[i], rest[through + 3 + i]
        step = source.shape[0] // PARTS
        parts = [pl.ds(j * step, step) for j in range(PARTS)]
        copies += start(rest[-1].at[i], *[(source.at[p], target.at[p]) for p in parts])
    mine_ref, hers_ref, out_ref = rest[through : through + 3]
    low = places[0] == 0
    one, one_decay, one_last, one_first = untagged(one_ref[...])
    two, _, two_last, _ = untagged(two_ref[...])
    two = jnp.where(places[places.shape[0] - 2] > 0, two, 0.0)
    facts = facts_ref[...]
    at_near = one + jnp.where(one_first == two_last, one_decay, 0.0) * two
    near_live = (facts[3:4] == one_last).astype(F32)
    near_decay, far_decay, far_live = facts[0:1] * near_live, facts[1:2], facts[2:3]
    at_far = (near_ref[...].astype(F32) + near_decay * at_near) * far_live
    at_near = at_near * near_live
    mine_ref[...] = jnp.where(low, at_near, at_far).astype(BF16)
    hers_ref[...] = jnp.where(low, at_far, at_near).astype(BF16)
    out_ref[...] = jnp.concatenate(
        [near_decay, far_decay, near_live, far_live, jnp.zeros((4, near_decay.shape[1]), F32)], axis=0
    )
    for copy in copies:
        copy.wait()


def pair_back_kernel(places, keep_ref, got_ref, facts_ref, _, tagged_ref, near_ref):
    low = places[0] == 0
    facts = facts_ref[...]
    keep, got = keep_ref[...].astype(F32), got_ref[...].astype(F32)
    near = jnp.where(low, got, keep) * facts[3:4]
    far = jnp.where(low, keep, got) * facts[2:3]
    half = near.shape[0]
    one = jnp.ones_like(facts[0:1])
    tagged_ref[:half, :] = (far + facts[0:1] * near).astype(BF16)
    tagged_ref[half:, :] = tags(facts[0:1] * facts[1:2], one, one)
    near_ref[...] = near.astype(BF16)


def enter_back_kernel(places, near_ref, facts_ref, one_ref, two_ref, _, mine_ref, hers_ref):
    low = places[0] == 0
    one, one_decay, one_last, one_first = untagged(one_ref[...])
    two, _, two_last, _ = untagged(two_ref[...])
    two = jnp.where(places[places.shape[0] - 1] > 0, two, 0.0)
    at_near = one + jnp.where(one_first == two_last, one_decay, 0.0) * two
    at_far = near_ref[...].astype(F32) + facts_ref[1:2, :] * at_near
    mine_ref[...] = jnp.where(low, at_far, at_near).astype(BF16)
    hers_ref[...] = jnp.where(low, at_near, at_far).astype(BF16)


def small(kernel, name, shapes, args, after, through=()):
    out_shape = [pltpu.VMEM(dims, kind) for dims, kind in shapes]
    out_shape += [pltpu.VMEM(a.shape, a.dtype) for a in through]
    return call(
        kernel, name, out_shape, [SM] + [VM] * len(args) + [HB] * len(through), (*args, after, *through),
        scratch=[pltpu.SemaphoreType.DMA((len(through), PARTS))] if through else (),
    )


def between_pairs(tagged, way):
    half = tagged.shape[0] - TILE
    window = max(lax.axis_size("seq") // 4, 1)
    if window <= 2:
        two = rotated(tagged, "seq", 4 * way) if window == 2 else jnp.zeros_like(tagged)
        return shifted(tagged, "seq", 2 * way), two
    total, decay, _, first = untagged(tagged)
    came, _, came_last, _ = untagged(shifted(tagged, "seq", 2 * way))
    decay = jnp.where(first == came_last, decay, 0.0)
    total = (total + decay * came).astype(BF16)
    reach = 2
    while reach < window:
        decay = decay * shifted(decay, "seq", way * reach)
        total = (total.astype(F32) + decay * shifted(total, "seq", 2 * way * reach).astype(F32)).astype(BF16)
        reach *= 2
    one = shifted(jnp.concatenate([total, tagged[half:]], axis=0), "seq", 2 * way)
    return one, jnp.zeros_like(one)


def shards(
    inputs, gates, write_keys, read_keys, log_decay, skip_gain, doc_ids, out_weight, grad_out
):
    tokens, inner = inputs.shape
    heads = log_decay.shape[0]
    width = inner // heads
    members = lax.axis_size("head")
    chips = members // 2
    chunk = tokens // members
    here = lax.axis_index("head")
    chip, core = here // 2, here % 2
    mate = here ^ 1
    side = lax.axis_index("seq") % 2
    numbers = [here, mate]
    for d in range(1, chips):
        source = (here - 2 * d) % members
        target = ((chip + d) % chips) * 2
        numbers += [source, source ^ 1, target + 1 - core, target + core]
    pair_at, pairs = lax.axis_index("seq") // 2, lax.axis_size("seq") // 2
    places = jnp.stack([side] + numbers + [pair_at >= 2, pair_at + 2 < pairs]).astype(jnp.int32)

    remote = [rotated(grad_out, "head", 2 * d) for d in range(1, chips)]
    sibling = swapped(grad_out, "head")
    mate_weight = swapped(out_weight, "head")

    spread = (
        jnp.arange(LANES)[:, None] == (jnp.arange(inner) // width)[None, :]
    ).astype(BF16)
    skip = jnp.repeat(skip_gain, width)[None, :]
    crow, entry, exit_w, local, keep, send, pre, blk, info, b, c = local_states(
        places, inputs, write_keys, read_keys, log_decay, doc_ids[None, :], spread
    )
    half, tagged, facts_shape = keep.shape, send.shape, info.shape
    mixed, gates, weight, own_grad = inside(
        places, inputs, b, c, crow, skip, heads, send, (gates, out_weight, grad_out)
    )
    pair, near, facts = small(
        pair_kernel, "pair", [(tagged, BF16), (half, BF16), (facts_shape, F32)],
        (places, keep, swapped(send, "seq"), info), mixed,
    )
    one, two = between_pairs(pair, 1)

    def grads(items, arrived, earlier, final, after, distant=False):
        return grad_chunks(
            chunk, items, places, arrived, gates, c, entry, pre, spread, weight, earlier, final, after,
            distant,
        )

    back = grads((1, 2), [own_grad, sibling], None, chips == 1, pair)
    part, mate_weight = inside(
        places, back[0], b, c, crow, skip, heads, back[1], (mate_weight,), which=(0, 1)
    )
    enter_keep, hers, facts, *remote = small(
        functools.partial(enter_kernel, len(remote)), "enter", [(half, BF16), (half, BF16), (facts_shape, F32)],
        (places, near, facts, one, two), part, remote,
    )
    enter_other = swapped(hers, "seq")

    def gated(items, *after):
        return gated_chunks(
            chunk, items, places, mixed, gates, c, entry, local, enter_keep, enter_other, pre, spread, after
        )

    for d in range(chips - 1):
        relayed = swapped(remote[d], "head")
        back = grads((3 + 4 * d,), [remote[d]], back, False, hers)
        back = grads((4 + 4 * d,), [relayed], back, d == chips - 2, back[1])
    mix, states, back_keep, back_send = back
    got = swapped(back_send, "seq")
    after, landed = back_send, []
    for d in range(chips - 1):
        give, stay = gated((5 + 4 * d, 6 + 4 * d), after)
        (after,) = project(stay, weight, None, F32, (give,), flops=FAR_COST)
        for total in project(swapped(give, "head"), mate_weight, after, BF16):
            landed.append(rotated(total, "head", 2 * (d + 1)))
            after = total
    pair, near = small(
        pair_back_kernel, "pair_back", [(tagged, BF16), (half, BF16)],
        (places, back_keep, got, facts), after,
    )
    one, two = between_pairs(pair, -1)
    give, stay = gated((2, 1), pair)
    (own,) = project(stay, weight, None, F32, (give,), flops=NEAR_COST)
    (own,) = project(swapped(give, "head"), mate_weight, own, F32)
    part = inside(places, mix, b, c, crow, skip, heads, own, which=(1, chips), earlier=part)[0]
    arrive_keep, hers = small(
        enter_back_kernel, "enter_back", [(half, BF16), (half, BF16)],
        (places, near, facts, one, two), part,
    )
    arrive_other = swapped(hers, "seq")
    out = chunk_sum(own, landed)
    grad_inputs = back_tail(
        places, part, b, exit_w, states, blk, arrive_keep, arrive_other, spread
    )
    return out, grad_inputs


def solution(mesh):
    in_specs = (
        P("seq", "head"),
        P("seq", "head"),
        P("seq", None),
        P("seq", None),
        P("head", "seq"),
        P("head"),
        P("seq"),
        P("head", None),
        P(("seq", "head"), None),
    )
    out_specs = (P(("seq", "head"), None), P("seq", "head"))
    return jax.shard_map(shards, mesh=mesh, in_specs=in_specs, out_specs=out_specs, check_vma=False)
```

```python
import functools
import math

import jax
import jax.numpy as jnp
from jax import lax
from jax.experimental import pallas as pl
from jax.experimental.pallas import tpu as pltpu
from jax.sharding import PartitionSpec as P

GROUP = 256
LANES = 128
TILE = 16
PARTS = 4
HALVES = 1
TAIL_COST, FAR_COST, NEAR_COST = 1.73e9, 2.306e10, 9.224e9
LOG2E = math.log2(math.e)
F32 = jnp.float32
BF16 = jnp.bfloat16
NT = (((1,), (1,)), ((), ()))
TN = (((0,), (0,)), ((), ()))
VM = pl.BlockSpec(memory_space=pltpu.VMEM)
SM = pl.BlockSpec(memory_space=pltpu.SMEM)
HB = pl.BlockSpec(memory_space=pltpu.HBM)
DECAY, DECAY_REST, LAST, FIRST = range(4)


def dot(a, b, dims=(((1,), (0,)), ((), ()))):
    return lax.dot_general(a, b, dims, preferred_element_type=F32)


def call(kernel, name, out_shape, in_specs, args, limit_mib=12, scratch=(), aliases=None, flops=1):
    space = {id(VM): pltpu.VMEM, id(HB): pltpu.HBM}
    args = [
        arg if spec is SM else pltpu.with_memory_space_constraint(arg, space[id(spec)])
        for spec, arg in zip(in_specs, args, strict=True)
    ]
    return pl.pallas_call(
        kernel,
        in_specs=in_specs,
        out_specs=[VM if o.memory_space == pltpu.VMEM else HB for o in out_shape],
        out_shape=out_shape,
        scratch_shapes=scratch,
        input_output_aliases=aliases or {},
        compiler_params=pltpu.CompilerParams(vmem_limit_bytes=limit_mib * 2**20),
        cost_estimate=pl.CostEstimate(flops=int(flops), bytes_accessed=1, transcendentals=0),
        name=name,
    )(*args)


def start(sems, *pairs):
    copies = [
        pltpu.make_async_copy(source, target, sems.at[i]) for i, (source, target) in enumerate(pairs)
    ]
    for copy in copies:
        copy.start()
    return copies


def split(value):
    high = value.astype(BF16)
    return high, (value - high.astype(F32)).astype(BF16)


def silu(gates):
    v = gates.astype(F32)
    return 0.5 * v * (1.0 + jnp.tanh(0.5 * v))


def row_at(rows, k):
    return jnp.sum(jnp.where(iota(rows.shape, 0) == k, rows, 0.0), axis=0, keepdims=True)


def iota(shape, dim):
    return lax.broadcasted_iota(jnp.int32, shape, dim)


def state_kernel(
    heads, blocks, places, x_hbm, b_hbm, c_hbm, ld_hbm, doc_hbm, spread_ref, *rest
):
    crow_ref, entry_ref, exit_ref, local_ref, keep_ref, send_ref, pre_ref, blk_ref, info_ref = rest[:9]
    b_ref, c_ref, padded, running, ld_ref, doc_ref, x_ref, sems = rest[9:]
    n, inner = running.shape
    half = n // 2
    parts = [pl.ds(k * GROUP, GROUP) for k in range(blocks)]
    ld_copy, doc_copy, b_copy, *x_copies, c_copy = start(
        sems, (ld_hbm, ld_ref), (doc_hbm, doc_ref), (b_hbm, b_ref),
        *[(x_hbm.at[p], x_ref.at[p]) for p in parts], (c_hbm, c_ref),
    )
    head_rows = crow_ref.shape[1]
    spread = spread_ref[...]
    later = (iota((GROUP, GROUP), 0) <= iota((GROUP, GROUP), 1)).astype(BF16)
    padded[...] = jnp.zeros_like(padded)
    row = iota((head_rows, GROUP), 0)
    states, ends, cols = [], [], []
    pre_ref[...] = jnp.zeros_like(pre_ref)
    blk_ref[...] = jnp.zeros_like(blk_ref)
    info_ref[...] = jnp.zeros_like(info_ref)
    ld_copy.wait()
    doc_copy.wait()
    for k in range(blocks):
        at = slice(k * GROUP, (k + 1) * GROUP)
        padded[k, 0:heads, :] = ld_ref[:, at] * LOG2E
    steps = jnp.concatenate([padded[k, 0:head_rows, :] for k in range(blocks)], axis=0)
    high, rest = split(steps)
    mid, low = split(steps - high.astype(F32))
    cum = dot(high, later) + (dot(mid, later) + dot(low, later))
    for k in range(blocks):
        at = slice(k * GROUP, (k + 1) * GROUP)
        own_cum = cum[k * head_rows : (k + 1) * head_rows]
        own_cum = jnp.where(row == head_rows - 1, doc_ref[:, at].astype(F32), own_cum)
        crow_ref[k] = own_cum
        padded[k, 0:head_rows, :] = own_cum
    b_copy.wait()
    for k in range(blocks):
        at = slice(k * GROUP, (k + 1) * GROUP)
        ccol = padded[k].T
        cols.append(ccol)
        docs = ccol[:, head_rows - 1 : head_rows]
        end = ccol[GROUP - 1 :]
        ends.append(end)
        end_doc = end[:, head_rows - 1 : head_rows]
        exit_w = jnp.where(docs == end_doc, jnp.exp2(jnp.minimum(end - ccol, 0.0)), 0.0).astype(BF16)
        exit_ref[at, :] = exit_w
        x_copies[k].wait()
        scaled = (dot(exit_w, spread) * x_ref[at, :].astype(F32)).astype(BF16)
        states.append(dot(b_ref[at, :], scaled, TN))
    doc_of = lambda line: line[:, head_rows - 1 : head_rows]
    first_doc = doc_of(cols[0][0:1])
    priors = [first_doc] + [doc_of(end) for end in ends[:-1]]
    last_doc = doc_of(ends[-1])
    total = jnp.zeros_like(ends[0])
    decays, prefixes = [], []
    for end, prior in zip(ends, priors):
        decays.append(jnp.where(doc_of(end) == prior, jnp.exp2(end), 0.0))
        total = total + end
        prefixes.append(jnp.where(doc_of(end) == first_doc, jnp.exp2(total), 0.0))
    stacked = decays + prefixes + [jnp.exp2(total)]
    stacked.append(jnp.zeros((-len(stacked) % 8, LANES), F32))
    high, rest = split(jnp.concatenate(stacked, axis=0))
    wide = dot(high, spread) + dot(rest, spread)
    blk_ref[0:blocks, :] = wide[0:blocks]
    pre_ref[0:1, :] = jnp.ones((1, inner), F32)
    pre_ref[1:blocks, :] = wide[blocks : 2 * blocks - 1]
    local_ref[0] = jnp.zeros((n, inner), BF16)
    now = states[0]
    for k in range(1, blocks):
        local_ref[k] = now.astype(BF16)
        now = wide[k : k + 1] * now + states[k]
    running[...] = now
    raw = wide[2 * blocks : 2 * blocks + 1]
    last_row = jnp.broadcast_to(last_doc + 1.0, (1, inner))
    first_row = jnp.broadcast_to(first_doc + 1.0, (1, inner))
    info_ref[0:1, :] = raw
    info_ref[1:2, :] = last_row
    info_ref[2:3, :] = first_row
    side = places[0]
    keep_ref[...] = running[pl.ds(pl.multiple_of(side * half, half), half), :].astype(BF16)
    send_ref[0:half, :] = running[pl.ds(pl.multiple_of((1 - side) * half, half), half), :].astype(BF16)
    send_ref[half:, :] = tags(raw, last_row, first_row)
    for k, prior in enumerate(priors):
        at = slice(k * GROUP, (k + 1) * GROUP)
        same = doc_of(cols[k]) == prior
        entry_ref[at, :] = jnp.where(same, jnp.exp2(jnp.minimum(cols[k], 0.0)), 0.0).astype(BF16)
    c_copy.wait()


def tags(decay, last, first):
    high, rest = split(decay)
    rows = [high.astype(F32), rest.astype(F32), last, first]
    rows.append(jnp.zeros((TILE - len(rows), decay.shape[1]), F32))
    return jnp.concatenate(rows, axis=0).astype(BF16)


def untagged(block):
    half = block.shape[0] - TILE
    state, rows = block[:half].astype(F32), block[half:].astype(F32)
    row = lambda i: rows[i : i + 1]
    return state, row(DECAY) + row(DECAY_REST), row(LAST), row(FIRST)


def local_states(places, inputs, write_keys, read_keys, log_decay, docs_row, spread):
    tokens, inner = inputs.shape
    heads = log_decay.shape[0]
    n = write_keys.shape[1]
    blocks = tokens // GROUP
    head_rows = -(-(heads + 1) // 8) * 8
    block_rows = -(-blocks // 8) * 8
    return call(
        functools.partial(state_kernel, heads, blocks),
        "local_states",
        [
            pltpu.VMEM((blocks, head_rows, GROUP), F32),
            pltpu.VMEM((tokens, LANES), BF16),
            pltpu.VMEM((tokens, LANES), BF16),
            pltpu.VMEM((blocks, n, inner), BF16),
            pltpu.VMEM((n // 2, inner), BF16),
            pltpu.VMEM((n // 2 + TILE, inner), BF16),
            pltpu.VMEM((block_rows, inner), F32),
            pltpu.VMEM((block_rows, inner), F32),
            pltpu.VMEM((8, inner), F32),
            pltpu.VMEM((tokens, n), BF16),
            pltpu.VMEM((tokens, n), BF16),
        ],
        [SM] + [HB] * 5 + [VM],
        (places, inputs, write_keys, read_keys, log_decay, docs_row, spread),
        scratch=[
            pltpu.VMEM((blocks, LANES, GROUP), F32),
            pltpu.VMEM((n, inner), F32),
            pltpu.VMEM((heads, tokens), F32),
            pltpu.VMEM((1, tokens), jnp.int32),
            pltpu.VMEM((tokens, inner), BF16),
            pltpu.SemaphoreType.DMA((4 + blocks,)),
        ],
    )


def inside_kernel(
    heads, width, blocks, backward, fetched, chips, which, places,
    x_ref, b_ref, c_ref, crow_ref, skip_ref, _, *rest
):
    per_chip = blocks // chips
    if backward and which[0]:
        rest = rest[1:]
    fetch_hbm, out_ref, fetch_vm, padded = (
        rest[:fetched], rest[fetched], rest[fetched + 1 : 2 * fetched + 1], rest[2 * fetched + 1]
    )
    half = GROUP // 2
    head_rows = crow_ref.shape[1]
    per = LANES // width
    part = lambda k: pl.ds(pl.multiple_of(k * GROUP, GROUP), GROUP)
    if not backward:
        x_sems, x_hbm, x_ref = rest[-2], x_ref, rest[-1]
        incoming = lambda k: pltpu.make_async_copy(x_hbm.at[part(k)], x_ref.at[part(k)], x_sems.at[k])
        for k in range(blocks):
            incoming(k).start()
    copies = start(rest[2 * fetched + 2], *zip(fetch_hbm, fetch_vm)) if fetched else []
    lane = iota((GROUP, LANES), 1)
    rows, cols = iota((GROUP, GROUP), 0), iota((GROUP, GROUP), 1)
    causal = (rows <= cols) if backward else (cols <= rows)
    padded[...] = jnp.zeros_like(padded)

    @pl.loop(which[0] * per_chip, which[1] * per_chip)
    def _(step):
        k = step
        if backward:
            turn = places[1] // 2 + step // per_chip
            k = lax.rem(turn, chips) * per_chip + lax.rem(step, per_chip)
        at = part(k)
        padded[0:head_rows, :] = crow_ref[k]
        col = padded[...].T
        docs_row = crow_ref[k, head_rows - 1 : head_rows, :]
        allowed = (col[:, head_rows - 1 : head_rows] == docs_row) & causal
        if backward:
            scores = dot(b_ref[at, :], c_ref[at, :], NT)
        else:
            scores = dot(c_ref[at, :], b_ref[at, :], NT)
        scores = jnp.where(allowed, scores, 0.0)
        if not backward:
            incoming(k).wait()
        for j in range(heads // per):
            cut = slice(j * LANES, (j + 1) * LANES)
            x = x_ref[at, cut]
            base = skip_ref[:, cut] * x.astype(F32)
            top, bottom = base[:half], base[half:]
            for i in range(per):
                h = j * per + i
                own = jnp.where(lane // width == i, x, jnp.zeros_like(x))
                at_row = crow_ref[k, h : h + 1, :]
                at_col = col[:, h : h + 1]

                def weights(r, c):
                    if backward:
                        gap = at_row[:, c] - at_col[r]
                    else:
                        gap = at_col[r] - at_row[:, c]
                    return (jnp.exp2(jnp.minimum(gap, 0.0)) * scores[r, c]).astype(BF16)

                low, high, both = slice(0, half), slice(half, GROUP), slice(0, GROUP)
                if backward:
                    top = top + dot(weights(low, both), own)
                    bottom = bottom + dot(weights(high, high), own[half:])
                else:
                    top = top + dot(weights(low, low), own[:half])
                    bottom = bottom + dot(weights(high, both), own)
            low_at = pl.ds(pl.multiple_of(k * GROUP, GROUP), half)
            high_at = pl.ds(pl.multiple_of(k * GROUP + half, half), half)
            out_ref[low_at, cut] = top.astype(BF16)
            out_ref[high_at, cut] = bottom.astype(BF16)

    for copy in copies:
        copy.wait()


def inside(places, x, write_keys, read_keys, crow, skip, heads, after, fetch=(), which=None, earlier=None):
    tokens, inner = x.shape
    blocks = tokens // GROUP
    backward = which is not None
    chips = lax.axis_size("head") // 2 if backward else 1
    carried = [] if earlier is None else [earlier]
    return call(
        functools.partial(
            inside_kernel, heads, inner // heads, blocks, backward, len(fetch), chips, which or (0, 1)
        ),
        "inside_backward" if backward else "inside_forward",
        [pltpu.VMEM((tokens, inner), BF16)] + [pltpu.VMEM(a.shape, a.dtype) for a in fetch],
        [SM] + [VM if backward else HB] + [VM] * (5 + len(carried)) + [HB] * len(fetch),
        (places, x, write_keys, read_keys, crow, skip, after, *carried, *fetch),
        scratch=[pltpu.VMEM((LANES, GROUP), F32)]
        + ([pltpu.SemaphoreType.DMA((len(fetch),))] if fetch else [])
        + ([] if backward else [
            pltpu.SemaphoreType.DMA((blocks,)),
            pltpu.VMEM((tokens, inner), BF16),
        ]),
        aliases={7: 0} if carried else None,
    )


def tiling(size):
    step = next(step for step in (512, 256, LANES, size) if size % step == 0)
    return [pl.ds(j * step, step) for j in range(size // step)]


def gate_kernel(
    items, chunk, places, mixed_ref, gates_ref, read_ref, entry_ref, local_ref,
    keep_ref, other_ref, pre_ref, spread_ref, *rest
):
    outs = rest[-len(items) :]
    at_low = places[0] == 0
    keep, other = keep_ref[...].astype(F32), other_ref[...].astype(F32)
    state = jnp.concatenate(
        [jnp.where(at_low, keep, other), jnp.where(at_low, other, keep)], axis=0
    )
    for item, out_ref in zip(items, outs):
        at = pl.ds(pl.multiple_of(places[item] * chunk, chunk), chunk)
        k = places[item] * chunk // GROUP
        entering = (local_ref[k].astype(F32) + row_at(pre_ref[...], k) * state).astype(BF16)
        carried = dot(read_ref[at, :], entering) * dot(entry_ref[at, :], spread_ref[...])
        out_ref[...] = (
            (mixed_ref[at, :].astype(F32) + carried) * silu(gates_ref[at, :])
        ).astype(BF16)


def gated_chunks(
    chunk, items, places, mixed, gates, read_keys, entry, local, keep, other, pre, spread, after
):
    inner = mixed.shape[1]
    return call(
        functools.partial(gate_kernel, items, chunk),
        "gated_chunks",
        [pltpu.VMEM((chunk, inner), BF16)] * len(items),
        [SM] + [VM] * (9 + len(after)),
        (places, mixed, gates, read_keys, entry, local, keep, other, pre, spread, *after),
    )


def project_kernel(has_part, count, gated_ref, w_ref, *rest):
    outs = rest[-count:]
    width = outs[0].shape[1]
    for i, out_ref in enumerate(outs):
        for cut in tiling(width):
            at = pl.ds(i * width + cut.start, cut.size)
            total = dot(gated_ref[...], w_ref[:, at])
            if has_part:
                total = rest[0][:, at] + total
            out_ref[:, cut] = total.astype(out_ref.dtype)


def project(gated, weight, part, kind, after=(), count=1, flops=1):
    shape = (gated.shape[0], weight.shape[1] // count)
    parts = [] if part is None else [part]
    return call(
        functools.partial(project_kernel, bool(parts), count),
        "project",
        [pltpu.VMEM(shape, kind)] * count,
        [VM] * (2 + len(parts) + len(after)),
        (gated, weight, *parts, *after),
        flops=flops,
    )


def sum_kernel(own_ref, *rest):
    landed_refs, (out_hbm, out_ref, sems) = rest[:-3], rest[-3:]
    outgoing = []
    width = landed_refs[0].shape[1] if landed_refs else own_ref.shape[1]
    for i in range(own_ref.shape[1] // width):
        at = pl.ds(i * width, width)
        total = own_ref[:, at]
        for ref in landed_refs[i :: own_ref.shape[1] // width]:
            total = total + ref[...].astype(F32)
        out_ref[:, at] = total.astype(BF16)
        outgoing += start(sems.at[i], (out_ref.at[:, at], out_hbm.at[:, at]))
    for copy in outgoing:
        copy.wait()


def chunk_sum(own, landed):
    return call(
        sum_kernel,
        "chunk_sum",
        [pltpu.HBM(own.shape, BF16)],
        [VM] * (1 + len(landed)),
        (own, *landed),
        scratch=[
            pltpu.VMEM(own.shape, BF16),
            pltpu.SemaphoreType.DMA((HALVES, 1)),
        ],
    )[0]


def grad_kernel(items, chunk, first, final, distant, places, *refs):
    count = len(items)
    go_refs, refs = refs[:count], refs[count:]
    if distant:
        go_ref, sems, refs = refs[-2], refs[-1], refs[:-2]
        for copy in start(sems, (go_refs[0], go_ref)):
            copy.wait()
        go_refs = [go_ref]
    gates_ref, read_ref, entry_ref, pre_ref, spread_ref, w_ref, _ = refs[:7]
    refs = refs[7:]
    if not first:
        sum_in, refs = refs[0], refs[3:]
    mix_ref, states_ref = refs[:2]
    summed = None if first else sum_in[...]
    for i, item in enumerate(items):
        at = pl.ds(pl.multiple_of(places[item] * chunk, chunk), chunk)
        k = places[item] * chunk // GROUP
        for cut in tiling(w_ref.shape[0]):
            grad = dot(go_refs[i][...], w_ref[cut, :], NT)
            mix_ref[at, cut] = (grad * silu(gates_ref[at, cut])).astype(BF16)
        scaled = (dot(entry_ref[at, :], spread_ref[...]) * mix_ref[at, :].astype(F32)).astype(BF16)
        state = dot(read_ref[at, :], scaled, TN)
        states_ref[places[item]] = state.astype(BF16)
        part = row_at(pre_ref[...], k) * state
        summed = part if summed is None else summed + part
    if final:
        half = summed.shape[0] // 2
        at_low = places[0] == 0
        refs[2][...] = jnp.where(at_low, summed[:half], summed[half:]).astype(BF16)
        refs[3][...] = jnp.where(at_low, summed[half:], summed[:half]).astype(BF16)
    else:
        refs[2][...] = summed


def grad_chunks(
    chunk, items, places, arrived, gates, read_keys, entry, pre, spread, out_weight, earlier, final, after,
    distant=False,
):
    count = len(arrived)
    inner = out_weight.shape[0]
    tokens = gates.shape[0]
    n = read_keys.shape[1]
    first = earlier is None
    out_shape = [pltpu.VMEM((tokens, inner), BF16), pltpu.VMEM((tokens // chunk, n, inner), BF16)]
    out_shape += [pltpu.VMEM((n // 2, inner), BF16)] * 2 if final else [pltpu.VMEM((n, inner), F32)]
    at = 1 + count + 7
    return call(
        functools.partial(grad_kernel, items, chunk, first, final, distant),
        "grad_chunks",
        out_shape,
        [SM] + [HB if distant else VM] * count + [VM] * (7 + (0 if first else 3)),
        (
            places, *arrived, gates, read_keys, entry, pre, spread, out_weight, after,
            *([] if first else (earlier[2], earlier[0], earlier[1])),
        ),
        scratch=[pltpu.VMEM(arrived[0].shape, BF16), pltpu.SemaphoreType.DMA((1,))] if distant else (),
        aliases=None if first else {at + 1: 0, at + 2: 1},
    )


def back_kernel(
    blocks, places, part_ref, b_ref, exit_ref, states_ref, blk_ref, keep_ref, other_ref, spread_ref,
    out_hbm, running, out_ref, out_sems,
):
    half = keep_ref.shape[0]
    per = states_ref.shape[0] // blocks
    side = places[0]
    running[pl.ds(pl.multiple_of(side * half, half), half), :] = keep_ref[...].astype(F32)
    running[pl.ds(pl.multiple_of((1 - side) * half, half), half), :] = other_ref[...].astype(F32)
    outgoing = []
    for k in reversed(range(blocks)):
        at = pl.ds(k * GROUP, GROUP)
        carried = dot(b_ref[at, :], running[...].astype(BF16)) * dot(exit_ref[at, :], spread_ref[...])
        out_ref[at, :] = (part_ref[at, :].astype(F32) + carried).astype(BF16)
        outgoing += start(out_sems.at[k], (out_ref.at[at], out_hbm.at[at]))
        if k:
            state = states_ref[k * per].astype(F32)
            for i in range(1, per):
                state = state + states_ref[k * per + i].astype(F32)
            running[...] = state + blk_ref[k : k + 1, :] * running[...]
    for copy in outgoing:
        copy.wait()


def back_tail(places, part, write_keys, exit_w, states, blk, keep, other, spread):
    tokens, inner = part.shape
    n = write_keys.shape[1]
    blocks = tokens // GROUP
    return call(
        functools.partial(back_kernel, blocks),
        "back_tail",
        [pltpu.HBM((tokens, inner), BF16)],
        [SM] + [VM] * 8,
        (places, part, write_keys, exit_w, states, blk, keep, other, spread),
        flops=TAIL_COST,
        scratch=[
            pltpu.VMEM((n, inner), F32),
            pltpu.VMEM((tokens, inner), BF16),
            pltpu.SemaphoreType.DMA((blocks, 1)),
        ],
    )[0]


def shifted(block, axis, distance):
    size = lax.axis_size(axis)
    route = [(i, i + distance) for i in range(size) if 0 <= i + distance < size]
    return lax.ppermute(block, axis, route)


def swapped(block, axis):
    return lax.ppermute(block, axis, [(i, i ^ 1) for i in range(lax.axis_size(axis))])


def rotated(block, axis, distance):
    size = lax.axis_size(axis)
    return lax.ppermute(block, axis, [(i, (i + distance) % size) for i in range(size)])


def pair_kernel(places, keep_ref, got_ref, info_ref, _, tagged_ref, near_ref, facts_ref):
    low = places[0] == 0
    pick = lambda own, mate: (jnp.where(low, own, mate), jnp.where(low, mate, own))
    got, mate_raw, mate_last, mate_first = untagged(got_ref[...])
    near, far = pick(keep_ref[...].astype(F32), got)
    near_raw, far_raw = pick(info_ref[0:1, :], mate_raw)
    near_last, far_last = pick(info_ref[1:2, :], mate_last)
    near_first, far_first = pick(info_ref[2:3, :], mate_first)
    far_live = (far_first == near_last).astype(F32)
    far_decay = jnp.where(far_last == far_first, far_raw, 0.0) * far_live
    near_decay = jnp.where(near_last == near_first, near_raw, 0.0)
    half = near.shape[0]
    tagged_ref[:half, :] = (far + far_decay * near).astype(BF16)
    tagged_ref[half:, :] = tags(far_decay * near_decay, far_last, near_first)
    near_ref[...] = near.astype(BF16)
    facts_ref[...] = jnp.concatenate(
        [near_decay, far_decay, far_live, near_first, jnp.zeros((4, near.shape[1]), F32)], axis=0
    )


def enter_kernel(through, places, near_ref, facts_ref, one_ref, two_ref, _, *rest):
    copies = []
    for i in range(through):
        source, target = rest[i], rest[through + 3 + i]
        step = source.shape[0] // PARTS
        parts = [pl.ds(j * step, step) for j in range(PARTS)]
        copies += start(rest[-1].at[i], *[(source.at[p], target.at[p]) for p in parts])
    mine_ref, hers_ref, out_ref = rest[through : through + 3]
    low = places[0] == 0
    one, one_decay, one_last, one_first = untagged(one_ref[...])
    two, _, two_last, _ = untagged(two_ref[...])
    two = jnp.where(places[places.shape[0] - 2] > 0, two, 0.0)
    facts = facts_ref[...]
    at_near = one + jnp.where(one_first == two_last, one_decay, 0.0) * two
    near_live = (facts[3:4] == one_last).astype(F32)
    near_decay, far_decay, far_live = facts[0:1] * near_live, facts[1:2], facts[2:3]
    at_far = (near_ref[...].astype(F32) + near_decay * at_near) * far_live
    at_near = at_near * near_live
    mine_ref[...] = jnp.where(low, at_near, at_far).astype(BF16)
    hers_ref[...] = jnp.where(low, at_far, at_near).astype(BF16)
    out_ref[...] = jnp.concatenate(
        [near_decay, far_decay, near_live, far_live, jnp.zeros((4, near_decay.shape[1]), F32)], axis=0
    )
    for copy in copies:
        copy.wait()


def pair_back_kernel(places, keep_ref, got_ref, facts_ref, _, tagged_ref, near_ref):
    low = places[0] == 0
    facts = facts_ref[...]
    keep, got = keep_ref[...].astype(F32), got_ref[...].astype(F32)
    near = jnp.where(low, got, keep) * facts[3:4]
    far = jnp.where(low, keep, got) * facts[2:3]
    half = near.shape[0]
    one = jnp.ones_like(facts[0:1])
    tagged_ref[:half, :] = (far + facts[0:1] * near).astype(BF16)
    tagged_ref[half:, :] = tags(facts[0:1] * facts[1:2], one, one)
    near_ref[...] = near.astype(BF16)


def enter_back_kernel(places, near_ref, facts_ref, one_ref, two_ref, _, mine_ref, hers_ref):
    low = places[0] == 0
    one, one_decay, one_last, one_first = untagged(one_ref[...])
    two, _, two_last, _ = untagged(two_ref[...])
    two = jnp.where(places[places.shape[0] - 1] > 0, two, 0.0)
    at_near = one + jnp.where(one_first == two_last, one_decay, 0.0) * two
    at_far = near_ref[...].astype(F32) + facts_ref[1:2, :] * at_near
    mine_ref[...] = jnp.where(low, at_far, at_near).astype(BF16)
    hers_ref[...] = jnp.where(low, at_near, at_far).astype(BF16)


def small(kernel, name, shapes, args, after, through=()):
    out_shape = [pltpu.VMEM(dims, kind) for dims, kind in shapes]
    out_shape += [pltpu.VMEM(a.shape, a.dtype) for a in through]
    return call(
        kernel, name, out_shape, [SM] + [VM] * len(args) + [HB] * len(through), (*args, after, *through),
        scratch=[pltpu.SemaphoreType.DMA((len(through), PARTS))] if through else (),
    )


def between_pairs(tagged, way):
    half = tagged.shape[0] - TILE
    window = max(lax.axis_size("seq") // 4, 1)
    if window <= 2:
        two = rotated(tagged, "seq", 4 * way) if window == 2 else jnp.zeros_like(tagged)
        return shifted(tagged, "seq", 2 * way), two
    total, decay, _, first = untagged(tagged)
    came, _, came_last, _ = untagged(shifted(tagged, "seq", 2 * way))
    decay = jnp.where(first == came_last, decay, 0.0)
    total = (total + decay * came).astype(BF16)
    reach = 2
    while reach < window:
        decay = decay * shifted(decay, "seq", way * reach)
        total = (total.astype(F32) + decay * shifted(total, "seq", 2 * way * reach).astype(F32)).astype(BF16)
        reach *= 2
    one = shifted(jnp.concatenate([total, tagged[half:]], axis=0), "seq", 2 * way)
    return one, jnp.zeros_like(one)


def shards(
    inputs, gates, write_keys, read_keys, log_decay, skip_gain, doc_ids, out_weight, grad_out
):
    tokens, inner = inputs.shape
    heads = log_decay.shape[0]
    width = inner // heads
    members = lax.axis_size("head")
    chips = members // 2
    chunk = tokens // members
    here = lax.axis_index("head")
    chip, core = here // 2, here % 2
    mate = here ^ 1
    side = lax.axis_index("seq") % 2
    numbers = [here, mate]
    for d in range(1, chips):
        source = (here - 2 * d) % members
        target = ((chip + d) % chips) * 2
        numbers += [source, source ^ 1, target + 1 - core, target + core]
    pair_at, pairs = lax.axis_index("seq") // 2, lax.axis_size("seq") // 2
    places = jnp.stack([side] + numbers + [pair_at >= 2, pair_at + 2 < pairs]).astype(jnp.int32)

    sibling = swapped(grad_out, "head")
    mate_weight = swapped(out_weight, "head")
    remote = [rotated(grad_out, "head", 2 * d) for d in range(1, chips)]

    spread = (
        jnp.arange(LANES)[:, None] == (jnp.arange(inner) // width)[None, :]
    ).astype(BF16)
    skip = jnp.repeat(skip_gain, width)[None, :]
    crow, entry, exit_w, local, keep, send, pre, blk, info, b, c = local_states(
        places, inputs, write_keys, read_keys, log_decay, doc_ids[None, :], spread
    )
    half, tagged, facts_shape = keep.shape, send.shape, info.shape
    mixed, gates, weight, own_grad = inside(
        places, inputs, b, c, crow, skip, heads, send, (gates, out_weight, grad_out)
    )
    pair, near, facts = small(
        pair_kernel, "pair", [(tagged, BF16), (half, BF16), (facts_shape, F32)],
        (places, keep, swapped(send, "seq"), info), mixed,
    )
    one, two = between_pairs(pair, 1)

    def grads(items, arrived, earlier, final, after, distant=False):
        return grad_chunks(
            chunk, items, places, arrived, gates, c, entry, pre, spread, weight, earlier, final, after,
            distant,
        )

    back = grads((1, 2), [own_grad, sibling], None, chips == 1, pair)
    part, mate_weight = inside(
        places, back[0], b, c, crow, skip, heads, back[1], (mate_weight,), which=(0, 1)
    )
    enter_keep, hers, facts, *remote = small(
        functools.partial(enter_kernel, len(remote)), "enter", [(half, BF16), (half, BF16), (facts_shape, F32)],
        (places, near, facts, one, two), part, remote,
    )
    enter_other = swapped(hers, "seq")

    def gated(items, *after):
        return gated_chunks(
            chunk, items, places, mixed, gates, c, entry, local, enter_keep, enter_other, pre, spread, after
        )

    for d in range(chips - 1):
        relayed = swapped(remote[d], "head")
        back = grads((3 + 4 * d,), [remote[d]], back, False, hers)
        back = grads((4 + 4 * d,), [relayed], back, d == chips - 2, back[1])
    mix, states, back_keep, back_send = back
    got = swapped(back_send, "seq")
    after, landed = back_send, []
    for d in range(chips - 1):
        give, stay = gated((5 + 4 * d, 6 + 4 * d), after)
        (after,) = project(stay, weight, None, F32, (give,), flops=FAR_COST)
        for total in project(swapped(give, "head"), mate_weight, after, BF16, count=HALVES):
            landed.append(rotated(total, "head", 2 * (d + 1)))
            after = total
    pair, near = small(
        pair_back_kernel, "pair_back", [(tagged, BF16), (half, BF16)],
        (places, back_keep, got, facts), after,
    )
    one, two = between_pairs(pair, -1)
    give, stay = gated((2, 1), pair)
    (own,) = project(stay, weight, None, F32, (give,), flops=NEAR_COST)
    (own,) = project(swapped(give, "head"), mate_weight, own, F32)
    part = inside(places, mix, b, c, crow, skip, heads, own, which=(1, chips), earlier=part)[0]
    arrive_keep, hers = small(
        enter_back_kernel, "enter_back", [(half, BF16), (half, BF16)],
        (places, near, facts, one, two), part,
    )
    arrive_other = swapped(hers, "seq")
    out = chunk_sum(own, landed)
    grad_inputs = back_tail(
        places, part, b, exit_w, states, blk, arrive_keep, arrive_other, spread
    )
    return out, grad_inputs


def solution(mesh):
    in_specs = (
        P("seq", "head"),
        P("seq", "head"),
        P("seq", None),
        P("seq", None),
        P("head", "seq"),
        P("head"),
        P("seq"),
        P("head", None),
        P(("seq", "head"), None),
    )
    out_specs = (P(("seq", "head"), None), P("seq", "head"))
    return jax.shard_map(shards, mesh=mesh, in_specs=in_specs, out_specs=out_specs, check_vma=False)
```
